32 devices in a mesh: tm: 16 (over z, y, core), sta: 2 (over x).
Axes of the slice: x: 2, y: 2, z: 4, core: 2. Of those that a mesh axis runs over, the one named last changes fastest.
Arguments:
- data: bfloat16 [64, 3, 6144], P('sta', None, 'tm'), as said below
- bank: bfloat16 [16, 8, 64, 3, 150], P('tm', None, 'sta'), may hold values from -6 to 6
- owners: int32 [2], replicated, may hold values from 0 to 15
- moveouts: int32 [2, 8, 64], P(None, None, 'sta'), may hold values from 0 to 64, as said below
Outputs:
- stack: float32 [2, 8, 6144], P(None, 'sta', 'tm')
The draws below stay inside these ranges and needn't reach their ends.
Inputs may be any that keep to these rules, and one draw needn't show every extreme that they name: `data`: three-component records with amplitudes that vary from station to station and along time. `moveouts`: delays are relative to the earliest arrival: for each template some station has 0 and some other station has 64.
All inputs are finite; a program needn't handle non-finite values.
Results may differ from the reference program's by a relative error of at most 0.0003.
Values may be sent and summed in bfloat16 or wider, within the bound.
A program may use at most 64 MiB of HBM per device.

```python
import math
import jax
import jax.numpy as jnp
from jax import lax

STA = 64
NTPL = 8
NB = 2
L = 150
MAXM = 64
NTIME = 6144
BANKS = 16
N_TM = 16


def draw_data(key, part):
    keys = jax.random.split(key, 2)
    shape = (STA, 3, NTIME)
    noise = jax.random.normal(keys[0], shape, jnp.float32)
    levels = jax.random.uniform(keys[1], (STA, 3, NTIME // 8), jnp.float32, 0.0, math.log(10.0))
    envelope = jnp.repeat(jnp.exp(levels), 8, axis=2)
    return (noise * envelope).astype(jnp.bfloat16)


def draw_moveouts(key, part):
    keys = jax.random.split(key, 3)
    delays = jax.random.randint(keys[0], (NB, NTPL, STA), 0, MAXM + 1)
    earliest = jax.random.randint(keys[1], (NB, NTPL, 1), 0, STA)
    stride = jax.random.randint(keys[2], (NB, NTPL, 1), 1, STA)
    farthest = (earliest + stride) % STA
    column = jnp.arange(STA, dtype=jnp.int32)[None, None, :]
    delays = jnp.where(column == earliest, 0, delays)
    delays = jnp.where(column == farthest, MAXM, delays)
    return delays.astype(jnp.int32)


def shard_levels(key, shape, pieces, smallest, high):
    gain = 1.0
    for position, shards_of in pieces:
        heights = jax.random.uniform(jax.random.fold_in(jax.random.fold_in(key, 6), position), (shards_of,), jnp.float32, smallest / len(pieces), high / len(pieces))
        gain = gain * jnp.repeat(jnp.exp(heights), shape[position] // shards_of).reshape((-1,) + (1,) * (len(shape) - 1 - position))
    return gain


def normal_values(rng, shape, width, limit, shards=(), kind=jnp.bfloat16):
    values = jax.random.normal(rng, shape, jnp.float32) * width
    if len(shards) > 0:
        values = shard_levels(rng, shape, shards, -0.22, 0.18) * values
    return jnp.clip(values, min=-limit, max=limit).astype(kind)


def setup_inputs(seed: int = 0) -> dict:
    key_list = jax.random.split(jax.random.key(seed), 5)
    return {
        "data": draw_data(jax.random.fold_in(key_list[4], 71), 0),
        "bank": normal_values(key_list[1], (BANKS, NTPL, STA, 3, L), 1.0, 6.0, ((0, 16), (2, 2))),
        "owners": jax.random.randint(key_list[2], (NB,), 0, N_TM).astype(jnp.int32),
        "moveouts": draw_moveouts(jax.random.fold_in(key_list[4], 71), 0),
    }


eps = 1e-06

def reference(data, bank, owners, moveouts):
    batches = jnp.take(bank, owners, axis=0)
    padded = jnp.pad(data, ((0, 0), (0, 0), (0, L - 1 + MAXM)))
    kernels = jnp.transpose(batches, (2, 0, 1, 3, 4)).reshape(STA, NB * NTPL, 3, L)
    delays = jnp.transpose(moveouts, (2, 0, 1)).reshape(STA, NB * NTPL)
    offsets = jnp.arange(NTIME, dtype=jnp.int32)

    def station_step(running, station_items):
        record, kernel, lag_row = station_items
        products = lax.conv_general_dilated(record[None], kernel, (1,), 'VALID', dimension_numbers=('NCH', 'OIH', 'NCH'), preferred_element_type=jnp.float32)[0]
        squares = lax.optimization_barrier(jnp.sum(jnp.square(record.astype(jnp.float32)), axis=0))
        energy = lax.reduce_window(squares, jnp.array(0.0, squares.dtype), lax.add, (L,), (1,), 'VALID') / (3 * L)
        tmpl_power = lax.optimization_barrier(jnp.sum(jnp.square(kernel.astype(jnp.float32)), axis=(1, 2))) / (3 * L)
        scores = products / (3 * L * jnp.sqrt(tmpl_power + eps)[:, None] * jnp.sqrt(energy + eps)[None, :])
        shifted = jnp.take_along_axis(scores, offsets[None, :] + lag_row.astype(jnp.int32)[:, None], axis=1)
        return (running + shifted, None)
    running, unused = lax.scan(station_step, jnp.zeros((NB * NTPL, NTIME), jnp.float32), (padded, kernels, delays))
    return running.reshape(NB, NTPL, NTIME)
```

```python
import functools

import jax
import jax.numpy as jnp
from jax import lax
from jax.experimental import pallas as pl
from jax.experimental.pallas import tpu as pltpu
from jax.sharding import PartitionSpec as P

MAXM = 64
SUB = 16
LANE = 128

eps = 1e-06


def round_up(value, unit):
    return (value + unit - 1) // unit * unit


def window_sums(values, span):
    width = values.shape[-1]

    def ahead(block, distance):
        return pltpu.roll(block, width - distance, axis=1)

    total, done, size, run = None, 0, 1, values
    parts = []
    while size <= span:
        parts.append((size, run))
        if 2 * size <= span:
            run = run + ahead(run, size)
        size *= 2
    for size, run in reversed(parts):
        if done + size <= span:
            piece = run if done == 0 else ahead(run, done)
            total = piece if total is None else total + piece
            done += size
    return total


def spread_kernel(
    blocks, slot_ref, owners_ref, out_ref, sums, core_in, a_near, a_far, b_far, b_near, send, recv
):
    comp_count, local_sta, tmpl_count, span = slot_ref.shape
    depth = round_up(span, SUB)
    lanes = out_ref.shape[2]
    batch_count = owners_ref.shape[0]
    columns = blocks // 4
    me = lax.axis_index("tm")
    core, row, column = me % 2, (me // 2) % 2, me // 4

    def place(at_column, at_row, at_core):
        return (at_column * 2 + at_row) * 2 + at_core

    core_peer = place(column, row, 1 - core)
    row_peer = place(column, 1 - row, core)
    far = [(column + step) % columns for step in range(1, columns)]
    far_peers = [place(other, row, core) for other in far]

    barrier = pltpu.get_barrier_semaphore()
    for peer in [core_peer, row_peer] + far_peers:
        pl.semaphore_signal(
            barrier, inc=1, device_id={"tm": peer}, device_id_type=pl.DeviceIdType.MESH
        )

    lag_at = lax.broadcasted_iota(jnp.int32, (span, lanes), 0)
    slot_at = lax.broadcasted_iota(jnp.int32, (span, lanes), 1)
    taps = jnp.zeros((local_sta * tmpl_count, lanes), jnp.float32)
    for comp in range(comp_count):
        flip = jnp.where(slot_at == (comp + 1) * depth - 1 - lag_at, 1.0, 0.0)
        block = slot_ref[comp].astype(jnp.float32).reshape(local_sta * tmpl_count, span)
        taps = taps + jnp.dot(
            block.astype(jnp.bfloat16),
            flip.astype(jnp.bfloat16),
            preferred_element_type=jnp.float32,
        )
    taps = taps.reshape(local_sta, tmpl_count, lanes)
    sums[...] = jnp.concatenate(
        [jnp.where(owners_ref[batch] == me, taps, 0.0) for batch in range(batch_count)], axis=1
    ).astype(jnp.bfloat16)

    pl.semaphore_wait(barrier, columns + 1)
    used = [0]

    def push(source, target, peer):
        slot = used[0]
        used[0] += 1
        copy = pltpu.make_async_remote_copy(
            src_ref=source,
            dst_ref=target,
            send_sem=send.at[slot],
            recv_sem=recv.at[slot],
            device_id={"tm": peer},
            device_id_type=pl.DeviceIdType.MESH,
        )
        copy.start()
        return copy

    half = local_sta // 2
    part = half // 2
    near, narrow = part // 2, part // columns
    one = near // columns
    base = core * half
    a_base, b_base = base, base + part

    copies = [push(sums.at[pl.ds((1 - core) * half, half)], core_in, core_peer)]
    copies[0].wait()
    mine = pl.ds(base, half)
    sums[mine] = sums[mine] + core_in[...]

    copies = [push(sums.at[pl.ds(a_base + (1 - row) * near, near)], a_near, row_peer)]
    for step in range(columns - 1):
        source = sums.at[pl.ds(b_base + far[step] * narrow, narrow)]
        copies.append(push(source, b_far.at[step], far_peers[step]))
    for copy in copies:
        copy.wait()
    a_mine = a_base + row * near
    b_mine = b_base + column * narrow
    sums[pl.ds(a_mine, near)] = sums[pl.ds(a_mine, near)] + a_near[...]
    total = sums[pl.ds(b_mine, narrow)]
    for step in range(columns - 1):
        total = total + b_far[step]
    sums[pl.ds(b_mine, narrow)] = total

    copies = [push(sums.at[pl.ds(b_mine + (1 - row) * one, one)], b_near, row_peer)]
    for step in range(columns - 1):
        source = sums.at[pl.ds(a_mine + far[step] * one, one)]
        copies.append(push(source, a_far.at[step], far_peers[step]))
    for copy in copies:
        copy.wait()
    a_one = pl.ds(a_mine + column * one, one)
    b_one = pl.ds(b_mine + row * one, one)
    out_ref[b_one] = sums[b_one] + b_near[...]
    total = sums[a_one]
    for step in range(columns - 1):
        total = total + a_far[step]
    out_ref[a_one] = total

    copies = [push(out_ref.at[b_one], out_ref.at[b_one], row_peer)]
    for peer in far_peers:
        copies.append(push(out_ref.at[a_one], out_ref.at[a_one], peer))
    for copy in copies:
        copy.wait()

    a_all, b_all = pl.ds(a_mine, near), pl.ds(b_mine, narrow)
    copies = [push(out_ref.at[a_all], out_ref.at[a_all], row_peer)]
    for peer in far_peers:
        copies.append(push(out_ref.at[b_all], out_ref.at[b_all], peer))
    for copy in copies:
        copy.wait()

    push(out_ref.at[mine], out_ref.at[mine], core_peer).wait()


def spread(slot, owners, blocks):
    comp_count, local_sta, tmpl_count, span = slot.shape
    row_count = owners.shape[0] * tmpl_count
    lanes = round_up(comp_count * round_up(span, SUB), LANE)
    columns = blocks // 4
    part = local_sta // 4
    tile = (row_count, lanes)
    count = 2 + 4 * columns
    return pl.pallas_call(
        functools.partial(spread_kernel, blocks),
        out_shape=jax.ShapeDtypeStruct((local_sta,) + tile, jnp.bfloat16),
        in_specs=[
            pl.BlockSpec(memory_space=pltpu.VMEM),
            pl.BlockSpec(memory_space=pltpu.SMEM),
        ],
        out_specs=pl.BlockSpec(memory_space=pltpu.VMEM),
        scratch_shapes=[
            pltpu.VMEM((local_sta,) + tile, jnp.bfloat16),
            pltpu.VMEM((local_sta // 2,) + tile, jnp.bfloat16),
            pltpu.VMEM((part // 2,) + tile, jnp.bfloat16),
            pltpu.VMEM((columns - 1, part // 2 // columns) + tile, jnp.bfloat16),
            pltpu.VMEM((columns - 1, part // columns) + tile, jnp.bfloat16),
            pltpu.VMEM((part // 2 // columns,) + tile, jnp.bfloat16),
            pltpu.SemaphoreType.DMA((count,)),
            pltpu.SemaphoreType.DMA((count,)),
        ],
        compiler_params=pltpu.CompilerParams(
            collective_id=0, has_side_effects=True, vmem_limit_bytes=32 * 1024 * 1024
        ),
    )(slot, owners)


def spread_by_sum(slot, owners):
    span = slot.shape[3]
    depth = round_up(span, SUB)
    position = lax.axis_index("tm")
    batches = [jnp.where(owners[b] == position, slot, 0) for b in range(owners.shape[0])]
    taps = lax.psum(jnp.concatenate(batches, axis=2), "tm")
    taps = jnp.pad(taps[..., ::-1], ((0, 0), (0, 0), (0, 0), (depth - span, 0)))
    taps = jnp.concatenate(list(taps), axis=2)
    lanes = round_up(taps.shape[2], LANE)
    return jnp.pad(taps, ((0, 0), (0, 0), (0, lanes - taps.shape[2])))


def correlate_kernel(span, stretch, data_ref, taps_ref, lag_ref, out_ref, rows, power):
    local_sta, comp_count, width = data_ref.shape
    _, row_count, lanes = taps_ref.shape
    depth = round_up(span, SUB)
    reach = round_up(stretch + MAXM, LANE)
    scale = 1.0 / (comp_count * span)

    squares = jnp.zeros((local_sta, width), jnp.float32)
    for comp in range(comp_count):
        block = data_ref[:, comp, :].astype(jnp.float32)
        rows[comp] = block
        squares = squares + block * block
    energy = window_sums(squares, span) * scale
    power[...] = (1.0 / jnp.sqrt(energy + eps))[:, :reach]

    def station(index, running):
        pieces = []
        for comp in range(comp_count):
            record = jnp.broadcast_to(rows[comp, pl.ds(index, 1), :], (SUB, width))
            frames = pltpu.roll(record, width - (SUB - 1), axis=1, stride=1, stride_axis=0)
            frames = frames.astype(jnp.bfloat16)
            for start in range(depth - SUB, -1, -SUB):
                moved = frames if start == 0 else pltpu.roll(frames, width - start, axis=1)
                pieces.append(moved[:, :reach])
        while len(pieces) * SUB < lanes:
            pieces.append(jnp.zeros((SUB, reach), jnp.bfloat16))
        taps = taps_ref[index]
        products = jnp.dot(
            taps, jnp.concatenate(pieces, axis=0), preferred_element_type=jnp.float32
        )
        squared = jnp.square(taps.astype(jnp.float32))
        tmpl_power = jnp.sum(squared, axis=1, keepdims=True) * scale
        tmpl_scale = scale / jnp.sqrt(tmpl_power + eps)
        scores = products * power[pl.ds(index, 1), :] * tmpl_scale
        lags = lag_ref[index]
        step = 1
        while step <= MAXM:
            chosen = jnp.broadcast_to((lags & step)[:, :1] != 0, scores.shape)
            scores = jnp.where(chosen, pltpu.roll(scores, reach - step, axis=1), scores)
            step *= 2
        return running + scores[:, :stretch]

    out_ref[...] = lax.fori_loop(
        0, local_sta, station, jnp.zeros((row_count, stretch), jnp.float32), unroll=2
    )


def meet(partial_sum):
    if lax.axis_size("sta") != 2:
        return lax.psum_scatter(partial_sum, "sta", scatter_dimension=1, tiled=True)
    kept = partial_sum.shape[1] // 2
    side = lax.axis_index("sta")
    other = lax.dynamic_slice_in_dim(partial_sum, (1 - side) * kept, kept, 1)
    own = lax.dynamic_slice_in_dim(partial_sum, side * kept, kept, 1)
    return own + lax.ppermute(other, "sta", [(0, 1), (1, 0)])


def shards(data, bank, owners, moveouts):
    local_sta, comp_count, stretch = data.shape
    span = bank.shape[-1]
    tmpl_count = bank.shape[1]
    batch_count = owners.shape[0]
    row_count = batch_count * tmpl_count
    blocks = lax.axis_size("tm")
    edge = span - 1 + MAXM
    width = round_up(stretch + MAXM + round_up(span, SUB), LANE)
    reach = round_up(stretch + MAXM, LANE)

    route = [(i + 1, i) for i in range(blocks - 1)]
    edge_cells = lax.ppermute(data[:, :, :edge], "tm", route)
    slot = jnp.transpose(bank[0], (2, 1, 0, 3))
    if blocks % 4 == 0 and local_sta % (2 * blocks) == 0 and row_count % SUB == 0:
        taps = spread(slot, owners, blocks)
    else:
        taps = spread_by_sum(slot, owners)
    window = jnp.concatenate([data, edge_cells], axis=2)
    window = jnp.pad(window, ((0, 0), (0, 0), (0, width - stretch - edge)))
    lags = jnp.transpose(moveouts, (2, 0, 1)).reshape(local_sta, row_count, 1)
    lags = jnp.broadcast_to(lags, (local_sta, row_count, LANE))

    partial_sum = pl.pallas_call(
        functools.partial(correlate_kernel, span, stretch),
        out_shape=jax.ShapeDtypeStruct((row_count, stretch), jnp.float32),
        in_specs=[pl.BlockSpec(memory_space=pltpu.VMEM)] * 3,
        out_specs=pl.BlockSpec(memory_space=pltpu.VMEM),
        scratch_shapes=[
            pltpu.VMEM((comp_count, local_sta, width), jnp.float32),
            pltpu.VMEM((local_sta, reach), jnp.float32),
        ],
        compiler_params=pltpu.CompilerParams(vmem_limit_bytes=32 * 1024 * 1024),
    )(window, taps, lags)
    return meet(partial_sum.reshape(batch_count, tmpl_count, stretch))


def solution(mesh):
    placed = (P("sta", None, "tm"), P("tm", None, "sta", None, None), P(), P(None, None, "sta"))
    return jax.shard_map(
        shards, mesh=mesh, in_specs=placed, out_specs=P(None, "sta", "tm"), check_vma=False
    )
```

```python
import functools

import jax
import jax.numpy as jnp
from jax import lax
from jax.experimental import pallas as pl
from jax.experimental.pallas import tpu as pltpu
from jax.sharding import PartitionSpec as P

MAXM = 64
SUB = 16
LANE = 128

eps = 1e-06


def round_up(value, unit):
    return (value + unit - 1) // unit * unit


def window_sums(values, span):
    width = values.shape[-1]

    def ahead(block, distance):
        return pltpu.roll(block, width - distance, axis=1)

    total, done, size, run = None, 0, 1, values
    parts = []
    while size <= span:
        parts.append((size, run))
        if 2 * size <= span:
            run = run + ahead(run, size)
        size *= 2
    for size, run in reversed(parts):
        if done + size <= span:
            piece = run if done == 0 else ahead(run, done)
            total = piece if total is None else total + piece
            done += size
    return total


def turned_taps(slot_ref, lanes):
    tmpl_count, comp_count, local_sta, span = slot_ref.shape
    depth = round_up(span, SUB)
    lag_at = lax.broadcasted_iota(jnp.int32, (span, lanes), 0)
    slot_at = lax.broadcasted_iota(jnp.int32, (span, lanes), 1)
    taps = jnp.zeros((tmpl_count * local_sta, lanes), jnp.float32)
    for comp in range(comp_count):
        flip = jnp.where(slot_at == (comp + 1) * depth - 1 - lag_at, 1.0, 0.0)
        block = slot_ref[:, comp].reshape(tmpl_count * local_sta, span)
        taps = taps + jnp.dot(
            block, flip.astype(jnp.bfloat16), preferred_element_type=jnp.float32
        )
    return jnp.swapaxes(taps.reshape(tmpl_count, local_sta, lanes), 0, 1)


def network_kernel(
    blocks,
    slot_ref,
    owners_ref,
    data_ref,
    moveouts_ref,
    out_ref,
    taps,
    sums,
    core_in,
    a_near,
    a_far,
    b_far,
    b_near,
    edge_in,
    rows,
    power,
    lags,
    frames,
    halves,
    half_in,
    send,
    recv,
):
    tmpl_count, comp_count, local_sta, span = slot_ref.shape
    lanes = taps.shape[2]
    stretch = data_ref.shape[2]
    width, reach = rows.shape[2], power.shape[1]
    batch_count = owners_ref.shape[0]
    row_count = batch_count * tmpl_count
    depth = round_up(span, SUB)
    scale = 1.0 / (comp_count * span)
    columns = blocks // 4
    me = lax.axis_index("tm")
    side = lax.axis_index("sta")
    core, row, column = me % 2, (me // 2) % 2, me // 4

    def place(at_column, at_row, at_core):
        return {"tm": (at_column * 2 + at_row) * 2 + at_core}

    core_peer = place(column, row, 1 - core)
    row_peer = place(column, 1 - row, core)
    far = [(column + step) % columns for step in range(1, columns)]
    far_peers = [place(other, row, core) for other in far]
    before, after = {"tm": (me + blocks - 1) % blocks}, {"tm": (me + 1) % blocks}
    sta_peer = {"sta": 1 - side}

    barrier = pltpu.get_barrier_semaphore()
    peers = [core_peer, row_peer, before, after, sta_peer] + far_peers
    for peer in peers:
        pl.semaphore_signal(
            barrier, inc=1, device_id=peer, device_id_type=pl.DeviceIdType.MESH
        )

    mine_taps = turned_taps(slot_ref, lanes)
    sums[...] = jnp.concatenate(
        [jnp.where(owners_ref[batch] == me, mine_taps, 0.0) for batch in range(batch_count)],
        axis=1,
    ).astype(jnp.bfloat16)

    pl.semaphore_wait(barrier, len(peers))
    used = [0]

    def push(source, target, peer):
        slot = used[0]
        used[0] += 1
        copy = pltpu.make_async_remote_copy(
            src_ref=source,
            dst_ref=target,
            send_sem=send.at[slot],
            recv_sem=recv.at[slot],
            device_id=peer,
            device_id_type=pl.DeviceIdType.MESH,
        )
        copy.start()
        return copy

    def build(index, unused):
        for comp in range(comp_count):
            record = jnp.broadcast_to(rows[comp, pl.ds(index, 1), :], (SUB, width))
            record = pltpu.roll(record, width - (SUB - 1), axis=1, stride=1, stride_axis=0)
            record = record.astype(jnp.bfloat16)
            moved = {0: record}
            for place_at in range(depth // SUB):
                start = depth - SUB - place_at * SUB
                shift, skip = start % LANE, start // LANE * LANE
                if shift not in moved:
                    moved[shift] = pltpu.roll(record, width - shift, axis=1)
                at = comp * depth + place_at * SUB
                frames[index, at : at + SUB, :] = moved[shift][:, skip : skip + reach]
        rest = lanes - comp_count * depth
        if rest > 0:
            frames[index, comp_count * depth :, :] = jnp.zeros((rest, reach), jnp.bfloat16)
        return unused

    def score(index, running):
        station_taps = taps[index]
        products = jnp.dot(station_taps, frames[index], preferred_element_type=jnp.float32)
        squared = jnp.square(station_taps.astype(jnp.float32))
        tmpl_power = jnp.sum(squared, axis=1, keepdims=True) * scale
        tmpl_scale = scale / jnp.sqrt(tmpl_power + eps)
        scores = products * power[pl.ds(index, 1), :] * tmpl_scale
        delays = lags[index]
        step = 1
        while step <= MAXM:
            chosen = jnp.broadcast_to((delays & step)[:, :1] != 0, scores.shape)
            scores = jnp.where(chosen, pltpu.roll(scores, reach - step, axis=1), scores)
            step *= 2
        return running + scores[:, :stretch]

    def build_some(first, last):
        lax.fori_loop(first, last, build, 0, unroll=2)

    def score_some(first, count, running):
        return lax.fori_loop(
            0, count, lambda i, held: score(first + i, held), running, unroll=min(count, 2)
        )

    half = local_sta // 2
    part = half // 2
    near, narrow = part // 2, part // columns
    one = near // columns
    base = core * half
    a_base, b_base = base, base + part
    mine = pl.ds(base, half)

    edge_copy = push(data_ref.at[:, :, pl.ds(0, edge_in.shape[2])], edge_in, before)
    copies = [push(sums.at[pl.ds((1 - core) * half, half)], core_in, core_peer)]
    delays = moveouts_ref[...]
    for station in range(local_sta):
        lags[station] = jnp.broadcast_to(delays[:, station : station + 1], (row_count, LANE))
    edge_copy.wait()
    squares = jnp.zeros((local_sta, width), jnp.float32)
    for comp in range(comp_count):
        edge = jnp.where(me == blocks - 1, 0.0, edge_in[comp].astype(jnp.float32))
        block = jnp.concatenate([data_ref[comp].astype(jnp.float32), edge], axis=1)[:, :width]
        rows[comp] = block
        squares = squares + block * block
    energy = window_sums(squares, span) * scale
    power[...] = (1.0 / jnp.sqrt(energy + eps))[:, :reach]
    copies[0].wait()
    sums[mine] = sums[mine] + core_in[...]

    copies = [push(sums.at[pl.ds(a_base + (1 - row) * near, near)], a_near, row_peer)]
    for step in range(columns - 1):
        source = sums.at[pl.ds(b_base + far[step] * narrow, narrow)]
        copies.append(push(source, b_far.at[step], far_peers[step]))
    build_some(0, half - 2)
    for copy in copies:
        copy.wait()
    a_mine = a_base + row * near
    b_mine = b_base + column * narrow
    sums[pl.ds(a_mine, near)] = sums[pl.ds(a_mine, near)] + a_near[...]
    total = sums[pl.ds(b_mine, narrow)]
    for step in range(columns - 1):
        total = total + b_far[step]
    sums[pl.ds(b_mine, narrow)] = total

    copies = [push(sums.at[pl.ds(b_mine + (1 - row) * one, one)], b_near, row_peer)]
    for step in range(columns - 1):
        source = sums.at[pl.ds(a_mine + far[step] * one, one)]
        copies.append(push(source, a_far.at[step], far_peers[step]))
    build_some(half - 2, half + part)
    for copy in copies:
        copy.wait()
    a_one, b_one = a_mine + column * one, b_mine + row * one
    a_two, b_two = pl.ds(a_one, one), pl.ds(b_one, one)
    taps[b_two] = sums[b_two] + b_near[...]
    total = sums[a_two]
    for step in range(columns - 1):
        total = total + a_far[step]
    taps[a_two] = total

    copies = [push(taps.at[b_two], taps.at[b_two], row_peer)]
    for peer in far_peers:
        copies.append(push(taps.at[a_two], taps.at[a_two], peer))
    build_some(half + part, local_sta)
    running = jnp.zeros((row_count, stretch), jnp.float32)
    for copy in copies:
        copy.wait()

    a_all, b_all = pl.ds(a_mine, near), pl.ds(b_mine, narrow)
    copies = [push(taps.at[a_all], taps.at[a_all], row_peer)]
    for peer in far_peers:
        copies.append(push(taps.at[b_all], taps.at[b_all], peer))
    running = score_some(a_mine, near, running)
    running = score_some(b_mine, narrow, running)
    for copy in copies:
        copy.wait()

    copies = [push(taps.at[mine], taps.at[mine], core_peer)]
    running = score_some(a_base + (1 - row) * near, near, running)
    for step in range(columns - 1):
        running = score_some(b_base + far[step] * narrow, narrow, running)
    copies[0].wait()
    running = score_some((1 - core) * half, half, running)

    kept = tmpl_count // 2
    for which in range(2):
        halves[which] = jnp.concatenate(
            [
                running[batch * tmpl_count + which * kept :][:kept]
                for batch in range(batch_count)
            ],
            axis=0,
        )
    copy = push(halves.at[1 - side], half_in, sta_peer)
    copy.wait()
    out_ref[...] = halves[side] + half_in[...]


def network(slot, owners, data, moveouts, blocks):
    tmpl_count, comp_count, local_sta, span = slot.shape
    stretch = data.shape[2]
    batch_count = owners.shape[0]
    row_count = batch_count * tmpl_count
    depth = round_up(span, SUB)
    lanes = round_up(comp_count * depth, LANE)
    width = round_up(stretch + MAXM + depth, LANE)
    reach = round_up(stretch + MAXM, LANE)
    columns = blocks // 4
    part = local_sta // 4
    tile = (row_count, lanes)
    count = 4 + 4 * columns
    kept = (row_count // 2, stretch)
    in_vmem = pl.BlockSpec(memory_space=pltpu.VMEM)
    return pl.pallas_call(
        functools.partial(network_kernel, blocks),
        out_shape=jax.ShapeDtypeStruct(kept, jnp.float32),
        in_specs=[in_vmem, pl.BlockSpec(memory_space=pltpu.SMEM), in_vmem, in_vmem],
        out_specs=in_vmem,
        scratch_shapes=[
            pltpu.VMEM((local_sta,) + tile, jnp.bfloat16),
            pltpu.VMEM((local_sta,) + tile, jnp.bfloat16),
            pltpu.VMEM((local_sta // 2,) + tile, jnp.bfloat16),
            pltpu.VMEM((part // 2,) + tile, jnp.bfloat16),
            pltpu.VMEM((columns - 1, part // 2 // columns) + tile, jnp.bfloat16),
            pltpu.VMEM((columns - 1, part // columns) + tile, jnp.bfloat16),
            pltpu.VMEM((part // 2 // columns,) + tile, jnp.bfloat16),
            pltpu.VMEM((comp_count, local_sta, width - stretch), jnp.bfloat16),
            pltpu.VMEM((comp_count, local_sta, width), jnp.float32),
            pltpu.VMEM((local_sta, reach), jnp.float32),
            pltpu.VMEM((local_sta, row_count, LANE), jnp.int32),
            pltpu.VMEM((local_sta, lanes, reach), jnp.bfloat16),
            pltpu.VMEM((2,) + kept, jnp.float32),
            pltpu.VMEM(kept, jnp.float32),
            pltpu.SemaphoreType.DMA((count,)),
            pltpu.SemaphoreType.DMA((count,)),
        ],
        compiler_params=pltpu.CompilerParams(
            collective_id=0, has_side_effects=True, vmem_limit_bytes=40 * 1024 * 1024
        ),
    )(slot, owners, data, moveouts)


def spread_by_sum(slot, owners):
    span = slot.shape[3]
    depth = round_up(span, SUB)
    position = lax.axis_index("tm")
    batches = [jnp.where(owners[b] == position, slot, 0) for b in range(owners.shape[0])]
    taps = lax.psum(jnp.concatenate(batches, axis=2), "tm")
    taps = jnp.pad(taps[..., ::-1], ((0, 0), (0, 0), (0, 0), (depth - span, 0)))
    taps = jnp.concatenate(list(taps), axis=2)
    lanes = round_up(taps.shape[2], LANE)
    return jnp.pad(taps, ((0, 0), (0, 0), (0, lanes - taps.shape[2])))


def correlate_kernel(span, stretch, data_ref, taps_ref, lag_ref, out_ref, rows, power):
    local_sta, comp_count, width = data_ref.shape
    _, row_count, lanes = taps_ref.shape
    depth = round_up(span, SUB)
    reach = round_up(stretch + MAXM, LANE)
    scale = 1.0 / (comp_count * span)

    squares = jnp.zeros((local_sta, width), jnp.float32)
    for comp in range(comp_count):
        block = data_ref[:, comp, :].astype(jnp.float32)
        rows[comp] = block
        squares = squares + block * block
    energy = window_sums(squares, span) * scale
    power[...] = (1.0 / jnp.sqrt(energy + eps))[:, :reach]

    def station(index, running):
        pieces = []
        for comp in range(comp_count):
            record = jnp.broadcast_to(rows[comp, pl.ds(index, 1), :], (SUB, width))
            frames = pltpu.roll(record, width - (SUB - 1), axis=1, stride=1, stride_axis=0)
            frames = frames.astype(jnp.bfloat16)
            for start in range(depth - SUB, -1, -SUB):
                moved = frames if start == 0 else pltpu.roll(frames, width - start, axis=1)
                pieces.append(moved[:, :reach])
        while len(pieces) * SUB < lanes:
            pieces.append(jnp.zeros((SUB, reach), jnp.bfloat16))
        taps = taps_ref[index]
        products = jnp.dot(
            taps, jnp.concatenate(pieces, axis=0), preferred_element_type=jnp.float32
        )
        squared = jnp.square(taps.astype(jnp.float32))
        tmpl_power = jnp.sum(squared, axis=1, keepdims=True) * scale
        tmpl_scale = scale / jnp.sqrt(tmpl_power + eps)
        scores = products * power[pl.ds(index, 1), :] * tmpl_scale
        lags = lag_ref[index]
        step = 1
        while step <= MAXM:
            chosen = jnp.broadcast_to((lags & step)[:, :1] != 0, scores.shape)
            scores = jnp.where(chosen, pltpu.roll(scores, reach - step, axis=1), scores)
            step *= 2
        return running + scores[:, :stretch]

    out_ref[...] = lax.fori_loop(
        0, local_sta, station, jnp.zeros((row_count, stretch), jnp.float32), unroll=2
    )


def fits(data, bank, owners):
    local_sta, _, stretch = data.shape
    blocks = lax.axis_size("tm")
    row_count = owners.shape[0] * bank.shape[1]
    reach = round_up(bank.shape[-1], SUB) + MAXM
    return (
        lax.axis_size("sta") == 2
        and blocks % 4 == 0
        and blocks > 4
        and local_sta % (2 * blocks) == 0
        and row_count % SUB == 0
        and bank.shape[1] % 2 == 0
        and stretch % LANE == 0
        and stretch >= round_up(reach, LANE)
    )


def shards(data, bank, owners, moveouts):
    local_sta, comp_count, stretch = data.shape
    span = bank.shape[-1]
    tmpl_count = bank.shape[1]
    batch_count = owners.shape[0]
    row_count = batch_count * tmpl_count
    blocks = lax.axis_size("tm")
    if fits(data, bank, owners):
        kept = network(
            jnp.transpose(bank[0], (0, 2, 1, 3)),
            owners,
            jnp.transpose(data, (1, 0, 2)),
            moveouts.reshape(row_count, local_sta),
            blocks,
        )
        return kept.reshape(batch_count, tmpl_count // 2, stretch)

    edge = span - 1 + MAXM
    width = round_up(stretch + MAXM + round_up(span, SUB), LANE)
    reach = round_up(stretch + MAXM, LANE)
    route = [(i + 1, i) for i in range(blocks - 1)]
    edge_cells = lax.ppermute(data[:, :, :edge], "tm", route)
    taps = spread_by_sum(jnp.transpose(bank[0], (2, 1, 0, 3)), owners)
    window = jnp.concatenate([data, edge_cells], axis=2)
    window = jnp.pad(window, ((0, 0), (0, 0), (0, width - stretch - edge)))
    lags = jnp.transpose(moveouts, (2, 0, 1)).reshape(local_sta, row_count, 1)
    lags = jnp.broadcast_to(lags, (local_sta, row_count, LANE))
    partial_sum = pl.pallas_call(
        functools.partial(correlate_kernel, span, stretch),
        out_shape=jax.ShapeDtypeStruct((row_count, stretch), jnp.float32),
        in_specs=[pl.BlockSpec(memory_space=pltpu.VMEM)] * 3,
        out_specs=pl.BlockSpec(memory_space=pltpu.VMEM),
        scratch_shapes=[
            pltpu.VMEM((comp_count, local_sta, width), jnp.float32),
            pltpu.VMEM((local_sta, reach), jnp.float32),
        ],
        compiler_params=pltpu.CompilerParams(vmem_limit_bytes=32 * 1024 * 1024),
    )(window, taps, lags)
    partial_sum = partial_sum.reshape(batch_count, tmpl_count, stretch)
    return lax.psum_scatter(partial_sum, "sta", scatter_dimension=1, tiled=True)


def solution(mesh):
    placed = (P("sta", None, "tm"), P("tm", None, "sta", None, None), P(), P(None, None, "sta"))
    return jax.shard_map(
        shards, mesh=mesh, in_specs=placed, out_specs=P(None, "sta", "tm"), check_vma=False
    )
```

```python
import functools

import jax
import jax.numpy as jnp
from jax import lax
from jax.experimental import pallas as pl
from jax.experimental.pallas import tpu as pltpu
from jax.sharding import PartitionSpec as P

MAXM = 64
SUB = 16
LANE = 128
PHASES = 4

eps = 1e-06


def round_up(value, unit):
    return (value + unit - 1) // unit * unit


def window_sums(values, span):
    width = values.shape[-1]

    def ahead(block, distance):
        return pltpu.roll(block, width - distance, axis=1)

    total, done, size, run = None, 0, 1, values
    parts = []
    while size <= span:
        parts.append((size, run))
        if 2 * size <= span:
            run = run + ahead(run, size)
        size *= 2
    for size, run in reversed(parts):
        if done + size <= span:
            piece = run if done == 0 else ahead(run, done)
            total = piece if total is None else total + piece
            done += size
    return total


def laid_taps(slot_ref, lanes):
    tmpl_count, comp_count, local_sta, span = slot_ref.shape
    depth = round_up(span, SUB)
    lag_at = lax.broadcasted_iota(jnp.int32, (span, lanes), 0)
    slot_at = lax.broadcasted_iota(jnp.int32, (span, lanes), 1)
    taps = jnp.zeros((tmpl_count * local_sta, lanes), jnp.float32)
    for comp in range(comp_count):
        laid = jnp.where(slot_at == comp * depth + lag_at, 1.0, 0.0)
        block = slot_ref[:, comp].reshape(tmpl_count * local_sta, span)
        taps = taps + jnp.dot(
            block, laid.astype(jnp.bfloat16), preferred_element_type=jnp.float32
        )
    return jnp.swapaxes(taps.reshape(tmpl_count, local_sta, lanes), 0, 1)


def ahead(block, distance):
    width = block.shape[-1]
    return block if distance == 0 else pltpu.roll(block, width - distance, axis=block.ndim - 1)


def phase_energies(squares, span):
    inner_last = span // PHASES
    groups = sum(squares[1:], squares[0])
    inner, size, done, run = None, 1, 1, groups
    length = inner_last - 1
    while size <= length:
        if length & size:
            piece = ahead(run, done)
            inner = piece if inner is None else inner + piece
            done += size
        run = run + ahead(run, size)
        size *= 2
    energies = []
    for phase in range(PHASES):
        total = inner
        for step in range(phase, phase + span):
            at, which = step // PHASES, step % PHASES
            if not 1 <= at < inner_last:
                total = total + ahead(squares[which], at)
        energies.append(total)
    return energies


def network_kernel(
    blocks,
    slot_hbm,
    owners_ref,
    data_hbm,
    moveouts_hbm,
    out_ref,
    slot_ref,
    data_ref,
    moveouts_ref,
    taps,
    sums,
    core_in,
    a_near,
    a_far,
    b_far,
    b_near,
    edge_in,
    rows,
    power,
    lags,
    frames,
    halves,
    half_in,
    local,
    send,
    recv,
):
    loads = [
        pltpu.make_async_copy(slot_hbm, slot_ref, local.at[0]),
        pltpu.make_async_copy(data_hbm, data_ref, local.at[1]),
        pltpu.make_async_copy(moveouts_hbm, moveouts_ref, local.at[2]),
    ]
    for load in loads:
        load.start()
    tmpl_count, comp_count, local_sta, span = slot_ref.shape
    lanes = taps.shape[2]
    stretch = data_ref.shape[2]
    width = stretch + edge_in.shape[2]
    batch_count = owners_ref.shape[0]
    row_count = batch_count * tmpl_count
    depth = round_up(span, SUB)
    scale = 1.0 / (comp_count * span)
    columns = blocks // 4
    me = lax.axis_index("tm")
    side = lax.axis_index("sta")
    core, row, column = me % 2, (me // 2) % 2, me // 4

    def place(at_column, at_row, at_core):
        return {"tm": (at_column * 2 + at_row) * 2 + at_core}

    core_peer = place(column, row, 1 - core)
    row_peer = place(column, 1 - row, core)
    far = [(column + step) % columns for step in range(1, columns)]
    far_peers = [place(other, row, core) for other in far]
    before, after = {"tm": (me + blocks - 1) % blocks}, {"tm": (me + 1) % blocks}
    sta_peer = {"sta": 1 - side}

    barrier = pltpu.get_barrier_semaphore()
    peers = [core_peer, row_peer, before, after, sta_peer] + far_peers
    for peer in peers:
        pl.semaphore_signal(
            barrier, inc=1, device_id=peer, device_id_type=pl.DeviceIdType.MESH
        )

    loads[0].wait()
    mine_taps = laid_taps(slot_ref, lanes)
    sums[...] = jnp.concatenate(
        [jnp.where(owners_ref[batch] == me, mine_taps, 0.0) for batch in range(batch_count)],
        axis=1,
    ).astype(jnp.bfloat16)

    pl.semaphore_wait(barrier, len(peers))
    used = [0]

    def push(source, target, peer):
        slot = used[0]
        used[0] += 1
        copy = pltpu.make_async_remote_copy(
            src_ref=source,
            dst_ref=target,
            send_sem=send.at[slot],
            recv_sem=recv.at[slot],
            device_id=peer,
            device_id_type=pl.DeviceIdType.MESH,
        )
        copy.start()
        return copy

    def build(index, unused):
        upper = lax.broadcasted_iota(jnp.int32, (2 * PHASES, 2 * LANE), 0) < PHASES
        for comp in range(comp_count):
            record = rows[comp * local_sta + index]
            groups = []
            for pair in range(SUB // (2 * PHASES)):
                groups.append(
                    jnp.where(upper, ahead(record, 2 * pair), ahead(record, 2 * pair + 1))
                )
            record = jnp.concatenate(groups, axis=0).astype(jnp.bfloat16)
            for group in range(depth // SUB):
                at = comp * depth + group * SUB
                frames[index, at : at + SUB, :] = ahead(record, group * SUB // PHASES)[:, :LANE]
        rest = lanes - comp_count * depth
        if rest > 0:
            frames[index, comp_count * depth :, :] = jnp.zeros((rest, LANE), jnp.bfloat16)
        return unused

    def score(index, running):
        station_taps = taps[index]
        moved = [station_taps]
        for phase in range(1, PHASES):
            moved.append(pltpu.roll(station_taps, phase, axis=1))
        products = jnp.dot(
            jnp.concatenate(moved, axis=0), frames[index], preferred_element_type=jnp.float32
        )
        squared = jnp.square(station_taps.astype(jnp.float32))
        tmpl_power = jnp.sum(squared, axis=1, keepdims=True) * scale
        tmpl_scale = scale / jnp.sqrt(tmpl_power + eps)
        scores = [
            products[phase * row_count : (phase + 1) * row_count]
            * power[phase, pl.ds(index, 1), :]
            * tmpl_scale
            for phase in range(PHASES)
        ]
        delays = lags[index]
        step = 1
        while step <= MAXM:
            chosen = (delays & step) != 0
            scores = [
                jnp.where(
                    chosen,
                    ahead(scores[(phase + step) % PHASES], (phase + step) // PHASES),
                    scores[phase],
                )
                for phase in range(PHASES)
            ]
            step *= 2
        return tuple(held + score for held, score in zip(running, scores))

    def build_some(first, last):
        lax.fori_loop(first, last, build, 0, unroll=2)

    def score_some(first, count, running):
        return lax.fori_loop(
            0, count, lambda i, held: score(first + i, held), running, unroll=min(count, 2)
        )

    half = local_sta // 2
    part = half // 2
    near, narrow = part // 2, part // columns
    one = near // columns
    base = core * half
    a_base, b_base = base, base + part
    mine = pl.ds(base, half)

    loads[1].wait()
    edge_copy = push(data_ref.at[:, :, pl.ds(0, edge_in.shape[2])], edge_in, before)
    copies = [push(sums.at[pl.ds((1 - core) * half, half)], core_in, core_peer)]
    loads[2].wait()
    delays = moveouts_ref[...]
    for station in range(local_sta):
        lags[station] = jnp.broadcast_to(delays[:, station : station + 1], (row_count, LANE))
    edge_copy.wait()
    pieces = []
    for comp in range(comp_count):
        edge = jnp.where(me == blocks - 1, 0.0, edge_in[comp].astype(jnp.float32))
        pieces.append(jnp.concatenate([data_ref[comp].astype(jnp.float32), edge], axis=1))
    window = jnp.concatenate(pieces, axis=0)
    time_at = lax.broadcasted_iota(jnp.int32, (width, 2 * LANE), 0)
    slot_at = lax.broadcasted_iota(jnp.int32, (width, 2 * LANE), 1)
    picked = jnp.where(time_at == PHASES * slot_at, 1.0, 0.0).astype(jnp.bfloat16)
    phased, squares = [], []
    for phase in range(PHASES):
        found = jnp.dot(
            ahead(window, phase).astype(jnp.bfloat16), picked, preferred_element_type=jnp.float32
        )
        phased.append(found)
        squares.append(
            sum(
                jnp.square(found[comp * local_sta : (comp + 1) * local_sta])
                for comp in range(comp_count)
            )
        )
    rows[...] = jnp.swapaxes(jnp.stack(phased + phased, axis=0), 0, 1)
    for phase, energy in enumerate(phase_energies(squares, span)):
        power[phase] = (1.0 / jnp.sqrt(energy * scale + eps))[:, :LANE]
    copies[0].wait()
    sums[mine] = sums[mine] + core_in[...]

    copies = [push(sums.at[pl.ds(a_base + (1 - row) * near, near)], a_near, row_peer)]
    for step in range(columns - 1):
        source = sums.at[pl.ds(b_base + far[step] * narrow, narrow)]
        copies.append(push(source, b_far.at[step], far_peers[step]))
    build_some(0, half)
    for copy in copies:
        copy.wait()
    a_mine = a_base + row * near
    b_mine = b_base + column * narrow
    sums[pl.ds(a_mine, near)] = sums[pl.ds(a_mine, near)] + a_near[...]
    total = sums[pl.ds(b_mine, narrow)]
    for step in range(columns - 1):
        total = total + b_far[step]
    sums[pl.ds(b_mine, narrow)] = total

    copies = [push(sums.at[pl.ds(b_mine + (1 - row) * one, one)], b_near, row_peer)]
    for step in range(columns - 1):
        source = sums.at[pl.ds(a_mine + far[step] * one, one)]
        copies.append(push(source, a_far.at[step], far_peers[step]))
    build_some(half, half + part + near)
    for copy in copies:
        copy.wait()
    a_one, b_one = a_mine + column * one, b_mine + row * one
    a_two, b_two = pl.ds(a_one, one), pl.ds(b_one, one)
    taps[b_two] = sums[b_two] + b_near[...]
    total = sums[a_two]
    for step in range(columns - 1):
        total = total + a_far[step]
    taps[a_two] = total

    copies = [push(taps.at[b_two], taps.at[b_two], row_peer)]
    for peer in far_peers:
        copies.append(push(taps.at[a_two], taps.at[a_two], peer))
    build_some(half + part + near, local_sta)
    running = (jnp.zeros((row_count, LANE), jnp.float32),) * PHASES
    for copy in copies:
        copy.wait()

    a_all, b_all = pl.ds(a_mine, near), pl.ds(b_mine, narrow)
    copies = [push(taps.at[a_all], taps.at[a_all], row_peer)]
    for peer in far_peers:
        copies.append(push(taps.at[b_all], taps.at[b_all], peer))
    running = score_some(a_mine, near, running)
    running = score_some(b_mine, narrow, running)
    for copy in copies:
        copy.wait()

    copies = [push(taps.at[mine], taps.at[mine], core_peer)]
    running = score_some(a_base + (1 - row) * near, near, running)
    for step in range(columns - 1):
        running = score_some(b_base + far[step] * narrow, narrow, running)
    copies[0].wait()
    running = score_some((1 - core) * half, half, running)

    kept = tmpl_count // 2
    for which in range(2):
        halves[which] = jnp.concatenate(
            [
                held[batch * tmpl_count + which * kept :][:kept]
                for held in running
                for batch in range(batch_count)
            ],
            axis=0,
        )
    copy = push(halves.at[1 - side], half_in, sta_peer)
    slot_at = lax.broadcasted_iota(jnp.int32, (LANE, stretch), 0)
    time_at = lax.broadcasted_iota(jnp.int32, (LANE, stretch), 1)
    copy.wait()
    summed = halves[side] + half_in[...]
    kept_rows = batch_count * kept
    result = jnp.zeros((kept_rows, stretch), jnp.float32)
    for phase in range(PHASES):
        placed = jnp.where(time_at == PHASES * slot_at + phase, 1.0, 0.0)
        result = result + jnp.dot(
            summed[phase * kept_rows : (phase + 1) * kept_rows],
            placed,
            precision=lax.Precision.HIGHEST,
            preferred_element_type=jnp.float32,
        )
    out_ref[...] = result


def network(slot, owners, data, moveouts, blocks):
    tmpl_count, comp_count, local_sta, span = slot.shape
    stretch = data.shape[2]
    batch_count = owners.shape[0]
    row_count = batch_count * tmpl_count
    depth = round_up(span, SUB)
    lanes = round_up(comp_count * depth, LANE)
    width = round_up(stretch + MAXM + depth, LANE)
    columns = blocks // 4
    part = local_sta // 4
    tile = (row_count, lanes)
    count = 4 + 4 * columns
    kept = (row_count // 2, stretch)
    phased = (PHASES * row_count // 2, LANE)
    anywhere = pl.BlockSpec(memory_space=pl.ANY)
    in_vmem = pl.BlockSpec(memory_space=pltpu.VMEM)
    return pl.pallas_call(
        functools.partial(network_kernel, blocks),
        out_shape=jax.ShapeDtypeStruct(kept, jnp.float32),
        in_specs=[anywhere, pl.BlockSpec(memory_space=pltpu.SMEM), anywhere, anywhere],
        out_specs=in_vmem,
        scratch_shapes=[
            pltpu.VMEM(slot.shape, slot.dtype),
            pltpu.VMEM(data.shape, data.dtype),
            pltpu.VMEM(moveouts.shape, moveouts.dtype),
            pltpu.VMEM((local_sta,) + tile, jnp.bfloat16),
            pltpu.VMEM((local_sta,) + tile, jnp.bfloat16),
            pltpu.VMEM((local_sta // 2,) + tile, jnp.bfloat16),
            pltpu.VMEM((part // 2,) + tile, jnp.bfloat16),
            pltpu.VMEM((columns - 1, part // 2 // columns) + tile, jnp.bfloat16),
            pltpu.VMEM((columns - 1, part // columns) + tile, jnp.bfloat16),
            pltpu.VMEM((part // 2 // columns,) + tile, jnp.bfloat16),
            pltpu.VMEM((comp_count, local_sta, width - stretch), jnp.bfloat16),
            pltpu.VMEM((comp_count * local_sta, 2 * PHASES, 2 * LANE), jnp.float32),
            pltpu.VMEM((PHASES, local_sta, LANE), jnp.float32),
            pltpu.VMEM((local_sta, row_count, LANE), jnp.int32),
            pltpu.VMEM((local_sta, lanes, LANE), jnp.bfloat16),
            pltpu.VMEM((2,) + phased, jnp.float32),
            pltpu.VMEM(phased, jnp.float32),
            pltpu.SemaphoreType.DMA((3,)),
            pltpu.SemaphoreType.DMA((count,)),
            pltpu.SemaphoreType.DMA((count,)),
        ],
        compiler_params=pltpu.CompilerParams(
            collective_id=0, has_side_effects=True, vmem_limit_bytes=60 * 1024 * 1024
        ),
    )(slot, owners, data, moveouts)


def spread_by_sum(slot, owners):
    span = slot.shape[3]
    depth = round_up(span, SUB)
    position = lax.axis_index("tm")
    batches = [jnp.where(owners[b] == position, slot, 0) for b in range(owners.shape[0])]
    taps = lax.psum(jnp.concatenate(batches, axis=2), "tm")
    taps = jnp.pad(taps[..., ::-1], ((0, 0), (0, 0), (0, 0), (depth - span, 0)))
    taps = jnp.concatenate(list(taps), axis=2)
    lanes = round_up(taps.shape[2], LANE)
    return jnp.pad(taps, ((0, 0), (0, 0), (0, lanes - taps.shape[2])))


def correlate_kernel(span, stretch, data_ref, taps_ref, lag_ref, out_ref, rows, power):
    local_sta, comp_count, width = data_ref.shape
    _, row_count, lanes = taps_ref.shape
    depth = round_up(span, SUB)
    reach = round_up(stretch + MAXM, LANE)
    scale = 1.0 / (comp_count * span)

    squares = jnp.zeros((local_sta, width), jnp.float32)
    for comp in range(comp_count):
        block = data_ref[:, comp, :].astype(jnp.float32)
        rows[comp] = block
        squares = squares + block * block
    energy = window_sums(squares, span) * scale
    power[...] = (1.0 / jnp.sqrt(energy + eps))[:, :reach]

    def station(index, running):
        pieces = []
        for comp in range(comp_count):
            record = jnp.broadcast_to(rows[comp, pl.ds(index, 1), :], (SUB, width))
            frames = pltpu.roll(record, width - (SUB - 1), axis=1, stride=1, stride_axis=0)
            frames = frames.astype(jnp.bfloat16)
            for start in range(depth - SUB, -1, -SUB):
                moved = frames if start == 0 else pltpu.roll(frames, width - start, axis=1)
                pieces.append(moved[:, :reach])
        while len(pieces) * SUB < lanes:
            pieces.append(jnp.zeros((SUB, reach), jnp.bfloat16))
        taps = taps_ref[index]
        products = jnp.dot(
            taps, jnp.concatenate(pieces, axis=0), preferred_element_type=jnp.float32
        )
        squared = jnp.square(taps.astype(jnp.float32))
        tmpl_power = jnp.sum(squared, axis=1, keepdims=True) * scale
        tmpl_scale = scale / jnp.sqrt(tmpl_power + eps)
        scores = products * power[pl.ds(index, 1), :] * tmpl_scale
        lags = lag_ref[index]
        step = 1
        while step <= MAXM:
            chosen = jnp.broadcast_to((lags & step)[:, :1] != 0, scores.shape)
            scores = jnp.where(chosen, pltpu.roll(scores, reach - step, axis=1), scores)
            step *= 2
        return running + scores[:, :stretch]

    out_ref[...] = lax.fori_loop(
        0, local_sta, station, jnp.zeros((row_count, stretch), jnp.float32), unroll=2
    )


def fits(data, bank, owners):
    local_sta, _, stretch = data.shape
    blocks = lax.axis_size("tm")
    row_count = owners.shape[0] * bank.shape[1]
    reach = round_up(bank.shape[-1], SUB) + MAXM
    return (
        lax.axis_size("sta") == 2
        and blocks % 4 == 0
        and blocks > 4
        and local_sta % (2 * blocks) == 0
        and row_count % SUB == 0
        and bank.shape[1] % 2 == 0
        and stretch % LANE == 0
        and stretch >= round_up(reach, LANE)
        and stretch + MAXM <= PHASES * LANE
        and bank.shape[1] // 2 * owners.shape[0] % 8 == 0
        and bank.shape[-1] >= 4 * PHASES
        and reach - MAXM <= PHASES * LANE
    )


def shards(data, bank, owners, moveouts):
    local_sta, comp_count, stretch = data.shape
    span = bank.shape[-1]
    tmpl_count = bank.shape[1]
    batch_count = owners.shape[0]
    row_count = batch_count * tmpl_count
    blocks = lax.axis_size("tm")
    if fits(data, bank, owners):
        kept = network(
            jnp.transpose(bank[0], (0, 2, 1, 3)),
            owners,
            jnp.transpose(data, (1, 0, 2)),
            moveouts.reshape(row_count, local_sta),
            blocks,
        )
        return kept.reshape(batch_count, tmpl_count // 2, stretch)

    edge = span - 1 + MAXM
    width = round_up(stretch + MAXM + round_up(span, SUB), LANE)
    reach = round_up(stretch + MAXM, LANE)
    route = [(i + 1, i) for i in range(blocks - 1)]
    edge_cells = lax.ppermute(data[:, :, :edge], "tm", route)
    taps = spread_by_sum(jnp.transpose(bank[0], (2, 1, 0, 3)), owners)
    window = jnp.concatenate([data, edge_cells], axis=2)
    window = jnp.pad(window, ((0, 0), (0, 0), (0, width - stretch - edge)))
    lags = jnp.transpose(moveouts, (2, 0, 1)).reshape(local_sta, row_count, 1)
    lags = jnp.broadcast_to(lags, (local_sta, row_count, LANE))
    partial_sum = pl.pallas_call(
        functools.partial(correlate_kernel, span, stretch),
        out_shape=jax.ShapeDtypeStruct((row_count, stretch), jnp.float32),
        in_specs=[pl.BlockSpec(memory_space=pltpu.VMEM)] * 3,
        out_specs=pl.BlockSpec(memory_space=pltpu.VMEM),
        scratch_shapes=[
            pltpu.VMEM((comp_count, local_sta, width), jnp.float32),
            pltpu.VMEM((local_sta, reach), jnp.float32),
        ],
        compiler_params=pltpu.CompilerParams(vmem_limit_bytes=32 * 1024 * 1024),
    )(window, taps, lags)
    partial_sum = partial_sum.reshape(batch_count, tmpl_count, stretch)
    return lax.psum_scatter(partial_sum, "sta", scatter_dimension=1, tiled=True)


def solution(mesh):
    placed = (P("sta", None, "tm"), P("tm", None, "sta", None, None), P(), P(None, None, "sta"))
    return jax.shard_map(
        shards, mesh=mesh, in_specs=placed, out_specs=P(None, "sta", "tm"), check_vma=False
    )
```

```python
import functools

import jax
import jax.numpy as jnp
from jax import lax
from jax.experimental import pallas as pl
from jax.experimental.pallas import tpu as pltpu
from jax.sharding import PartitionSpec as P

MAXM = 64
SUB = 16
LANE = 128
PHASES = 4

eps = 1e-06


def round_up(value, unit):
    return (value + unit - 1) // unit * unit


def window_sums(values, span):
    width = values.shape[-1]

    def ahead(block, distance):
        return pltpu.roll(block, width - distance, axis=1)

    total, done, size, run = None, 0, 1, values
    parts = []
    while size <= span:
        parts.append((size, run))
        if 2 * size <= span:
            run = run + ahead(run, size)
        size *= 2
    for size, run in reversed(parts):
        if done + size <= span:
            piece = run if done == 0 else ahead(run, done)
            total = piece if total is None else total + piece
            done += size
    return total


def laid_taps(slot_ref, lanes):
    tmpl_count, comp_count, local_sta, span = slot_ref.shape
    depth = round_up(span, SUB)
    lag_at = lax.broadcasted_iota(jnp.int32, (span, lanes), 0)
    slot_at = lax.broadcasted_iota(jnp.int32, (span, lanes), 1)
    taps = jnp.zeros((tmpl_count * local_sta, lanes), jnp.float32)
    for comp in range(comp_count):
        laid = jnp.where(slot_at == comp * depth + lag_at, 1.0, 0.0)
        block = slot_ref[:, comp].reshape(tmpl_count * local_sta, span)
        taps = taps + jnp.dot(
            block, laid.astype(jnp.bfloat16), preferred_element_type=jnp.float32
        )
    return jnp.swapaxes(taps.reshape(tmpl_count, local_sta, lanes), 0, 1)


def ahead(block, distance):
    width = block.shape[-1]
    return block if distance == 0 else pltpu.roll(block, width - distance, axis=block.ndim - 1)


def phase_energies(squares, span):
    inner_last = span // PHASES
    groups = sum(squares[1:], squares[0])
    inner, size, done, run = None, 1, 1, groups
    length = inner_last - 1
    while size <= length:
        if length & size:
            piece = ahead(run, done)
            inner = piece if inner is None else inner + piece
            done += size
        run = run + ahead(run, size)
        size *= 2
    energies = []
    for phase in range(PHASES):
        total = inner
        for step in range(phase, phase + span):
            at, which = step // PHASES, step % PHASES
            if not 1 <= at < inner_last:
                total = total + ahead(squares[which], at)
        energies.append(total)
    return energies


def network_kernel(
    blocks,
    slot_hbm,
    owners_ref,
    data_hbm,
    moveouts_hbm,
    out_ref,
    slot_ref,
    data_ref,
    moveouts_ref,
    taps,
    parcels,
    inbox,
    edge_in,
    rows,
    power,
    lags,
    frames,
    halves,
    half_in,
    local,
    send,
    recv,
):
    loads = [
        pltpu.make_async_copy(slot_hbm, slot_ref, local.at[0]),
        pltpu.make_async_copy(data_hbm, data_ref, local.at[1]),
        pltpu.make_async_copy(moveouts_hbm, moveouts_ref, local.at[2]),
    ]
    for load in loads:
        load.start()
    tmpl_count, comp_count, local_sta, span = slot_ref.shape
    lanes = taps.shape[2]
    stretch = data_ref.shape[2]
    width = stretch + edge_in.shape[2]
    batch_count = owners_ref.shape[0]
    row_count = batch_count * tmpl_count
    depth = round_up(span, SUB)
    scale = 1.0 / (comp_count * span)
    columns = blocks // 4
    me = lax.axis_index("tm")
    side = lax.axis_index("sta")
    core, row, column = me % 2, (me // 2) % 2, me // 4

    def place(at_column, at_row, at_core):
        return {"tm": (at_column * 2 + at_row) * 2 + at_core}

    core_peer = place(column, row, 1 - core)
    row_peer = place(column, 1 - row, core)
    far = [(column + step) % columns for step in range(1, columns)]
    far_peers = [place(other, row, core) for other in far]
    others = [(me + step) % blocks for step in range(1, blocks)]
    sta_peer = {"sta": 1 - side}

    barrier = pltpu.get_barrier_semaphore()
    peers = [sta_peer] + [{"tm": other} for other in others]
    for peer in peers:
        pl.semaphore_signal(
            barrier, inc=1, device_id=peer, device_id_type=pl.DeviceIdType.MESH
        )

    loads[0].wait()
    mine_taps = laid_taps(slot_ref, lanes)
    half = local_sta // 2
    part = half // 2
    near, narrow = part // 2, part // columns
    for other in range(blocks):
        at_core, at_row, at_column = other % 2, (other // 2) % 2, other // 4
        a_at = at_core * half + at_row * near + at_column
        b_at = at_core * half + part + at_column * narrow + at_row
        parcels[other] = jnp.concatenate([mine_taps[a_at], mine_taps[b_at]], axis=0).astype(
            jnp.bfloat16
        )

    pl.semaphore_wait(barrier, len(peers))
    used = [0]

    def push(source, target, peer):
        slot = used[0]
        used[0] += 1
        copy = pltpu.make_async_remote_copy(
            src_ref=source,
            dst_ref=target,
            send_sem=send.at[slot],
            recv_sem=recv.at[slot],
            device_id=peer,
            device_id_type=pl.DeviceIdType.MESH,
        )
        copy.start()
        return copy

    def build(index, unused):
        upper = lax.broadcasted_iota(jnp.int32, (2 * PHASES, 2 * LANE), 0) < PHASES
        for comp in range(comp_count):
            record = rows[comp * local_sta + index]
            groups = []
            for pair in range(SUB // (2 * PHASES)):
                groups.append(
                    jnp.where(upper, ahead(record, 2 * pair), ahead(record, 2 * pair + 1))
                )
            record = jnp.concatenate(groups, axis=0).astype(jnp.bfloat16)
            for group in range(depth // SUB):
                at = comp * depth + group * SUB
                frames[index, at : at + SUB, :] = ahead(record, group * SUB // PHASES)[:, :LANE]
        rest = lanes - comp_count * depth
        if rest > 0:
            frames[index, comp_count * depth :, :] = jnp.zeros((rest, LANE), jnp.bfloat16)
        return unused

    def score(index, running):
        station_taps = taps[index]
        moved = [station_taps]
        for phase in range(1, PHASES):
            moved.append(pltpu.roll(station_taps, phase, axis=1))
        products = jnp.dot(
            jnp.concatenate(moved, axis=0), frames[index], preferred_element_type=jnp.float32
        )
        squared = jnp.square(station_taps.astype(jnp.float32))
        tmpl_power = jnp.sum(squared, axis=1, keepdims=True) * scale
        tmpl_scale = scale / jnp.sqrt(tmpl_power + eps)
        scores = [
            products[phase * row_count : (phase + 1) * row_count]
            * power[phase, pl.ds(index, 1), :]
            * tmpl_scale
            for phase in range(PHASES)
        ]
        delays = lags[index]
        step = 1
        while step <= MAXM:
            chosen = (delays & step) != 0
            scores = [
                jnp.where(
                    chosen,
                    ahead(scores[(phase + step) % PHASES], (phase + step) // PHASES),
                    scores[phase],
                )
                for phase in range(PHASES)
            ]
            step *= 2
        return tuple(held + score for held, score in zip(running, scores))

    def build_some(first, last):
        lax.fori_loop(first, last, build, 0, unroll=2)

    def score_some(first, count, running):
        return lax.fori_loop(
            0, count, lambda i, held: score(first + i, held), running, unroll=min(count, 2)
        )

    base = core * half
    a_base, b_base = base, base + part
    mine = pl.ds(base, half)

    copies = [push(parcels.at[other], inbox.at[me], {"tm": other}) for other in others]
    loads[1].wait()
    edge_copy = push(data_ref.at[:, :, pl.ds(0, edge_in.shape[2])], edge_in, {"tm": others[-1]})
    loads[2].wait()
    delays = moveouts_ref[...]
    for station in range(local_sta):
        lags[station] = jnp.broadcast_to(delays[:, station : station + 1], (row_count, LANE))
    edge_copy.wait()
    pieces = []
    for comp in range(comp_count):
        edge = jnp.where(me == blocks - 1, 0.0, edge_in[comp].astype(jnp.float32))
        pieces.append(jnp.concatenate([data_ref[comp].astype(jnp.float32), edge], axis=1))
    window = jnp.concatenate(pieces, axis=0)
    time_at = lax.broadcasted_iota(jnp.int32, (width, 2 * LANE), 0)
    slot_at = lax.broadcasted_iota(jnp.int32, (width, 2 * LANE), 1)
    picked = jnp.where(time_at == PHASES * slot_at, 1.0, 0.0).astype(jnp.bfloat16)
    phased, squares = [], []
    for phase in range(PHASES):
        found = jnp.dot(
            ahead(window, phase).astype(jnp.bfloat16), picked, preferred_element_type=jnp.float32
        )
        phased.append(found)
        squares.append(
            sum(
                jnp.square(found[comp * local_sta : (comp + 1) * local_sta])
                for comp in range(comp_count)
            )
        )
    rows[...] = jnp.swapaxes(jnp.stack(phased + phased, axis=0), 0, 1)
    for phase, energy in enumerate(phase_energies(squares, span)):
        power[phase] = (1.0 / jnp.sqrt(energy * scale + eps))[:, :LANE]
    build_some(0, half + part + near)
    inbox[me] = parcels[me]
    for copy in copies:
        copy.wait()
    a_mine = a_base + row * near
    b_mine = b_base + column * narrow
    a_one, b_one = a_mine + column, b_mine + row
    a_two, b_two = pl.ds(a_one, 1), pl.ds(b_one, 1)
    chosen = [inbox[owners_ref[batch]].astype(jnp.float32) for batch in range(batch_count)]
    for at, skip in ((a_one, 0), (b_one, tmpl_count)):
        taps[at] = jnp.concatenate(
            [held[skip : skip + tmpl_count] for held in chosen], axis=0
        ).astype(jnp.bfloat16)

    copies = [push(taps.at[b_two], taps.at[b_two], row_peer)]
    for peer in far_peers:
        copies.append(push(taps.at[a_two], taps.at[a_two], peer))
    build_some(half + part + near, local_sta)
    running = (jnp.zeros((row_count, LANE), jnp.float32),) * PHASES
    for copy in copies:
        copy.wait()

    a_all, b_all = pl.ds(a_mine, near), pl.ds(b_mine, narrow)
    copies = [push(taps.at[a_all], taps.at[a_all], row_peer)]
    for peer in far_peers:
        copies.append(push(taps.at[b_all], taps.at[b_all], peer))
    early = [push(taps.at[held], taps.at[held], core_peer) for held in (a_all, b_all)]
    running = score_some(a_mine, near, running)
    running = score_some(b_mine, narrow, running)
    for copy in early:
        copy.wait()
    twin = (1 - core) * half
    running = score_some(twin + row * near, near, running)
    running = score_some(twin + part + column * narrow, narrow, running)
    for copy in copies:
        copy.wait()

    a_rest = (1 - row) * near
    rest = [(a_rest, near)] + [(part + other * narrow, narrow) for other in far]
    late = []
    for first, count in rest:
        held = pl.ds(base + first, count)
        late.append(push(taps.at[held], taps.at[held], core_peer))
    for first, count in rest:
        running = score_some(base + first, count, running)
    for copy in late:
        copy.wait()
    for first, count in rest:
        running = score_some(twin + first, count, running)

    kept = tmpl_count // 2
    for which in range(2):
        halves[which] = jnp.concatenate(
            [
                held[batch * tmpl_count + which * kept :][:kept]
                for held in running
                for batch in range(batch_count)
            ],
            axis=0,
        )
    copy = push(halves.at[1 - side], half_in, sta_peer)
    slot_at = lax.broadcasted_iota(jnp.int32, (LANE, stretch), 0)
    time_at = lax.broadcasted_iota(jnp.int32, (LANE, stretch), 1)
    copy.wait()
    summed = halves[side] + half_in[...]
    kept_rows = batch_count * kept
    result = jnp.zeros((kept_rows, stretch), jnp.float32)
    for phase in range(PHASES):
        placed = jnp.where(time_at == PHASES * slot_at + phase, 1.0, 0.0)
        result = result + jnp.dot(
            summed[phase * kept_rows : (phase + 1) * kept_rows],
            placed,
            precision=lax.Precision.HIGHEST,
            preferred_element_type=jnp.float32,
        )
    out_ref[...] = result


def network(slot, owners, data, moveouts, blocks):
    tmpl_count, comp_count, local_sta, span = slot.shape
    stretch = data.shape[2]
    batch_count = owners.shape[0]
    row_count = batch_count * tmpl_count
    depth = round_up(span, SUB)
    lanes = round_up(comp_count * depth, LANE)
    width = round_up(stretch + MAXM + depth, LANE)
    columns = blocks // 4
    tile = (row_count, lanes)
    count = blocks + 2 + 2 * columns + 2 + columns
    kept = (row_count // 2, stretch)
    phased = (PHASES * row_count // 2, LANE)
    anywhere = pl.BlockSpec(memory_space=pl.ANY)
    in_vmem = pl.BlockSpec(memory_space=pltpu.VMEM)
    return pl.pallas_call(
        functools.partial(network_kernel, blocks),
        out_shape=jax.ShapeDtypeStruct(kept, jnp.float32),
        in_specs=[anywhere, pl.BlockSpec(memory_space=pltpu.SMEM), anywhere, anywhere],
        out_specs=in_vmem,
        scratch_shapes=[
            pltpu.VMEM(slot.shape, slot.dtype),
            pltpu.VMEM(data.shape, data.dtype),
            pltpu.VMEM(moveouts.shape, moveouts.dtype),
            pltpu.VMEM((local_sta,) + tile, jnp.bfloat16),
            pltpu.VMEM((blocks,) + tile, jnp.bfloat16),
            pltpu.VMEM((blocks,) + tile, jnp.bfloat16),
            pltpu.VMEM((comp_count, local_sta, width - stretch), jnp.bfloat16),
            pltpu.VMEM((comp_count * local_sta, 2 * PHASES, 2 * LANE), jnp.float32),
            pltpu.VMEM((PHASES, local_sta, LANE), jnp.float32),
            pltpu.VMEM((local_sta, row_count, LANE), jnp.int32),
            pltpu.VMEM((local_sta, lanes, LANE), jnp.bfloat16),
            pltpu.VMEM((2,) + phased, jnp.float32),
            pltpu.VMEM(phased, jnp.float32),
            pltpu.SemaphoreType.DMA((3,)),
            pltpu.SemaphoreType.DMA((count,)),
            pltpu.SemaphoreType.DMA((count,)),
        ],
        compiler_params=pltpu.CompilerParams(
            collective_id=0, has_side_effects=True, vmem_limit_bytes=60 * 1024 * 1024
        ),
    )(slot, owners, data, moveouts)


def spread_by_sum(slot, owners):
    span = slot.shape[3]
    depth = round_up(span, SUB)
    position = lax.axis_index("tm")
    batches = [jnp.where(owners[b] == position, slot, 0) for b in range(owners.shape[0])]
    taps = lax.psum(jnp.concatenate(batches, axis=2), "tm")
    taps = jnp.pad(taps[..., ::-1], ((0, 0), (0, 0), (0, 0), (depth - span, 0)))
    taps = jnp.concatenate(list(taps), axis=2)
    lanes = round_up(taps.shape[2], LANE)
    return jnp.pad(taps, ((0, 0), (0, 0), (0, lanes - taps.shape[2])))


def correlate_kernel(span, stretch, data_ref, taps_ref, lag_ref, out_ref, rows, power):
    local_sta, comp_count, width = data_ref.shape
    _, row_count, lanes = taps_ref.shape
    depth = round_up(span, SUB)
    reach = round_up(stretch + MAXM, LANE)
    scale = 1.0 / (comp_count * span)

    squares = jnp.zeros((local_sta, width), jnp.float32)
    for comp in range(comp_count):
        block = data_ref[:, comp, :].astype(jnp.float32)
        rows[comp] = block
        squares = squares + block * block
    energy = window_sums(squares, span) * scale
    power[...] = (1.0 / jnp.sqrt(energy + eps))[:, :reach]

    def station(index, running):
        pieces = []
        for comp in range(comp_count):
            record = jnp.broadcast_to(rows[comp, pl.ds(index, 1), :], (SUB, width))
            frames = pltpu.roll(record, width - (SUB - 1), axis=1, stride=1, stride_axis=0)
            frames = frames.astype(jnp.bfloat16)
            for start in range(depth - SUB, -1, -SUB):
                moved = frames if start == 0 else pltpu.roll(frames, width - start, axis=1)
                pieces.append(moved[:, :reach])
        while len(pieces) * SUB < lanes:
            pieces.append(jnp.zeros((SUB, reach), jnp.bfloat16))
        taps = taps_ref[index]
        products = jnp.dot(
            taps, jnp.concatenate(pieces, axis=0), preferred_element_type=jnp.float32
        )
        squared = jnp.square(taps.astype(jnp.float32))
        tmpl_power = jnp.sum(squared, axis=1, keepdims=True) * scale
        tmpl_scale = scale / jnp.sqrt(tmpl_power + eps)
        scores = products * power[pl.ds(index, 1), :] * tmpl_scale
        lags = lag_ref[index]
        step = 1
        while step <= MAXM:
            chosen = jnp.broadcast_to((lags & step)[:, :1] != 0, scores.shape)
            scores = jnp.where(chosen, pltpu.roll(scores, reach - step, axis=1), scores)
            step *= 2
        return running + scores[:, :stretch]

    out_ref[...] = lax.fori_loop(
        0, local_sta, station, jnp.zeros((row_count, stretch), jnp.float32), unroll=2
    )


def fits(data, bank, owners):
    local_sta, _, stretch = data.shape
    blocks = lax.axis_size("tm")
    row_count = owners.shape[0] * bank.shape[1]
    reach = round_up(bank.shape[-1], SUB) + MAXM
    return (
        lax.axis_size("sta") == 2
        and blocks % 4 == 0
        and blocks > 4
        and local_sta == 2 * blocks
        and row_count == SUB
        and owners.shape[0] == 2
        and bank.shape[1] % 2 == 0
        and stretch % LANE == 0
        and stretch >= round_up(reach, LANE)
        and stretch + MAXM <= PHASES * LANE
        and bank.shape[1] // 2 * owners.shape[0] % 8 == 0
        and bank.shape[-1] >= 4 * PHASES
        and reach - MAXM <= PHASES * LANE
    )


def shards(data, bank, owners, moveouts):
    local_sta, comp_count, stretch = data.shape
    span = bank.shape[-1]
    tmpl_count = bank.shape[1]
    batch_count = owners.shape[0]
    row_count = batch_count * tmpl_count
    blocks = lax.axis_size("tm")
    if fits(data, bank, owners):
        kept = network(
            jnp.transpose(bank[0], (0, 2, 1, 3)),
            owners,
            jnp.transpose(data, (1, 0, 2)),
            moveouts.reshape(row_count, local_sta),
            blocks,
        )
        return kept.reshape(batch_count, tmpl_count // 2, stretch)

    edge = span - 1 + MAXM
    width = round_up(stretch + MAXM + round_up(span, SUB), LANE)
    reach = round_up(stretch + MAXM, LANE)
    route = [(i + 1, i) for i in range(blocks - 1)]
    edge_cells = lax.ppermute(data[:, :, :edge], "tm", route)
    taps = spread_by_sum(jnp.transpose(bank[0], (2, 1, 0, 3)), owners)
    window = jnp.concatenate([data, edge_cells], axis=2)
    window = jnp.pad(window, ((0, 0), (0, 0), (0, width - stretch - edge)))
    lags = jnp.transpose(moveouts, (2, 0, 1)).reshape(local_sta, row_count, 1)
    lags = jnp.broadcast_to(lags, (local_sta, row_count, LANE))
    partial_sum = pl.pallas_call(
        functools.partial(correlate_kernel, span, stretch),
        out_shape=jax.ShapeDtypeStruct((row_count, stretch), jnp.float32),
        in_specs=[pl.BlockSpec(memory_space=pltpu.VMEM)] * 3,
        out_specs=pl.BlockSpec(memory_space=pltpu.VMEM),
        scratch_shapes=[
            pltpu.VMEM((comp_count, local_sta, width), jnp.float32),
            pltpu.VMEM((local_sta, reach), jnp.float32),
        ],
        compiler_params=pltpu.CompilerParams(vmem_limit_bytes=32 * 1024 * 1024),
    )(window, taps, lags)
    partial_sum = partial_sum.reshape(batch_count, tmpl_count, stretch)
    return lax.psum_scatter(partial_sum, "sta", scatter_dimension=1, tiled=True)


def solution(mesh):
    placed = (P("sta", None, "tm"), P("tm", None, "sta", None, None), P(), P(None, None, "sta"))
    return jax.shard_map(
        shards, mesh=mesh, in_specs=placed, out_specs=P(None, "sta", "tm"), check_vma=False
    )
```

```python
import functools

import jax
import jax.numpy as jnp
from jax import lax
from jax.experimental import pallas as pl
from jax.experimental.pallas import tpu as pltpu
from jax.sharding import PartitionSpec as P

MAXM = 64
SUB = 16
LANE = 128
PHASES = 4

eps = 1e-06


def round_up(value, unit):
    return (value + unit - 1) // unit * unit


def window_sums(values, span):
    width = values.shape[-1]

    def ahead(block, distance):
        return pltpu.roll(block, width - distance, axis=1)

    total, done, size, run = None, 0, 1, values
    parts = []
    while size <= span:
        parts.append((size, run))
        if 2 * size <= span:
            run = run + ahead(run, size)
        size *= 2
    for size, run in reversed(parts):
        if done + size <= span:
            piece = run if done == 0 else ahead(run, done)
            total = piece if total is None else total + piece
            done += size
    return total


def laid_taps(slot_ref, lanes):
    tmpl_count, comp_count, local_sta, span = slot_ref.shape
    depth = round_up(span, SUB)
    lag_at = lax.broadcasted_iota(jnp.int32, (span, lanes), 0)
    slot_at = lax.broadcasted_iota(jnp.int32, (span, lanes), 1)
    taps = jnp.zeros((tmpl_count * local_sta, lanes), jnp.float32)
    for comp in range(comp_count):
        laid = jnp.where(slot_at == comp * depth + lag_at, 1.0, 0.0)
        block = slot_ref[:, comp].reshape(tmpl_count * local_sta, span)
        taps = taps + jnp.dot(
            block, laid.astype(jnp.bfloat16), preferred_element_type=jnp.float32
        )
    return jnp.swapaxes(taps.reshape(tmpl_count, local_sta, lanes), 0, 1)


def ahead(block, distance):
    width = block.shape[-1]
    return block if distance == 0 else pltpu.roll(block, width - distance, axis=block.ndim - 1)


def phase_energies(squares, span):
    inner_last = span // PHASES
    groups = sum(squares[1:], squares[0])
    inner, size, done, run = None, 1, 1, groups
    length = inner_last - 1
    while size <= length:
        if length & size:
            piece = ahead(run, done)
            inner = piece if inner is None else inner + piece
            done += size
        run = run + ahead(run, size)
        size *= 2
    energies = []
    for phase in range(PHASES):
        total = inner
        for step in range(phase, phase + span):
            at, which = step // PHASES, step % PHASES
            if not 1 <= at < inner_last:
                total = total + ahead(squares[which], at)
        energies.append(total)
    return energies


def network_kernel(
    blocks,
    slot_hbm,
    owners_ref,
    data_hbm,
    moveouts_hbm,
    out_ref,
    slot_ref,
    data_ref,
    moveouts_ref,
    taps,
    parcels,
    inbox,
    edge_in,
    rows,
    power,
    lags,
    frames,
    halves,
    half_in,
    local,
    send,
    recv,
):
    loads = [
        pltpu.make_async_copy(slot_hbm, slot_ref, local.at[0]),
        pltpu.make_async_copy(data_hbm, data_ref, local.at[1]),
        pltpu.make_async_copy(moveouts_hbm, moveouts_ref, local.at[2]),
    ]
    for load in loads:
        load.start()
    tmpl_count, comp_count, local_sta, span = slot_ref.shape
    lanes = taps.shape[2]
    stretch = data_ref.shape[2]
    width = stretch + edge_in.shape[2]
    batch_count = owners_ref.shape[0]
    row_count = batch_count * tmpl_count
    depth = round_up(span, SUB)
    scale = 1.0 / (comp_count * span)
    columns = blocks // 4
    me = lax.axis_index("tm")
    side = lax.axis_index("sta")
    core, row, column = me % 2, (me // 2) % 2, me // 4

    def place(at_column, at_row, at_core):
        return {"tm": (at_column * 2 + at_row) * 2 + at_core}

    core_peer = place(column, row, 1 - core)
    row_peer = place(column, 1 - row, core)
    far = [(column + step) % columns for step in range(1, columns)]
    far_peers = [place(other, row, core) for other in far]
    steps = sorted(range(1, blocks), key=lambda step: abs(2 * step - blocks))
    others = [(me + step) % blocks for step in steps]
    before = {"tm": (me + blocks - 1) % blocks}
    sta_peer = {"sta": 1 - side}

    barrier = pltpu.get_barrier_semaphore()
    peers = [sta_peer] + [{"tm": other} for other in others]
    for peer in peers:
        pl.semaphore_signal(
            barrier, inc=1, device_id=peer, device_id_type=pl.DeviceIdType.MESH
        )

    loads[0].wait()
    mine_taps = laid_taps(slot_ref, lanes)
    half = local_sta // 2
    part = half // 2
    near, narrow = part // 2, part // columns
    for other in range(blocks):
        at_core, at_row, at_column = other % 2, (other // 2) % 2, other // 4
        a_at = at_core * half + at_row * near + at_column
        b_at = at_core * half + part + at_column * narrow + at_row
        parcels[other] = jnp.concatenate([mine_taps[a_at], mine_taps[b_at]], axis=0).astype(
            jnp.bfloat16
        )

    pl.semaphore_wait(barrier, len(peers))
    used = [0]

    def push(source, target, peer):
        slot = used[0]
        used[0] += 1
        copy = pltpu.make_async_remote_copy(
            src_ref=source,
            dst_ref=target,
            send_sem=send.at[slot],
            recv_sem=recv.at[slot],
            device_id=peer,
            device_id_type=pl.DeviceIdType.MESH,
        )
        copy.start()
        return copy

    def build(index, unused):
        upper = lax.broadcasted_iota(jnp.int32, (2 * PHASES, 2 * LANE), 0) < PHASES
        for comp in range(comp_count):
            record = rows[comp * local_sta + index]
            groups = []
            for pair in range(SUB // (2 * PHASES)):
                groups.append(
                    jnp.where(upper, ahead(record, 2 * pair), ahead(record, 2 * pair + 1))
                )
            record = jnp.concatenate(groups, axis=0).astype(jnp.bfloat16)
            for group in range(depth // SUB):
                at = comp * depth + group * SUB
                frames[index, at : at + SUB, :] = ahead(record, group * SUB // PHASES)[:, :LANE]
        rest = lanes - comp_count * depth
        if rest > 0:
            frames[index, comp_count * depth :, :] = jnp.zeros((rest, LANE), jnp.bfloat16)
        return unused

    def score(index, running):
        station_taps = taps[index]
        moved = [station_taps]
        for phase in range(1, PHASES):
            moved.append(pltpu.roll(station_taps, phase, axis=1))
        products = jnp.dot(
            jnp.concatenate(moved, axis=0), frames[index], preferred_element_type=jnp.float32
        )
        squared = jnp.square(station_taps.astype(jnp.float32))
        tmpl_power = jnp.sum(squared, axis=1, keepdims=True) * scale
        tmpl_scale = scale / jnp.sqrt(tmpl_power + eps)
        scores = [
            products[phase * row_count : (phase + 1) * row_count]
            * power[phase, pl.ds(index, 1), :]
            * tmpl_scale
            for phase in range(PHASES)
        ]
        delays = lags[index]
        step = 1
        while step <= MAXM:
            chosen = (delays & step) != 0
            scores = [
                jnp.where(
                    chosen,
                    ahead(scores[(phase + step) % PHASES], (phase + step) // PHASES),
                    scores[phase],
                )
                for phase in range(PHASES)
            ]
            step *= 2
        return tuple(held + score for held, score in zip(running, scores))

    def build_some(first, last):
        lax.fori_loop(first, last, build, 0, unroll=2)

    def score_some(first, count, running):
        return lax.fori_loop(
            0, count, lambda i, held: score(first + i, held), running, unroll=min(count, 2)
        )

    base = core * half
    a_base, b_base = base, base + part

    loads[1].wait()
    edge_copy = push(data_ref.at[:, :, pl.ds(0, edge_in.shape[2])], edge_in, before)
    copies = [push(parcels.at[other], inbox.at[me], {"tm": other}) for other in others]
    loads[2].wait()
    delays = moveouts_ref[...]
    for station in range(local_sta):
        lags[station] = jnp.broadcast_to(delays[:, station : station + 1], (row_count, LANE))
    edge_copy.wait()
    pieces = []
    for comp in range(comp_count):
        edge = jnp.where(me == blocks - 1, 0.0, edge_in[comp].astype(jnp.float32))
        pieces.append(jnp.concatenate([data_ref[comp].astype(jnp.float32), edge], axis=1))
    window = jnp.concatenate(pieces, axis=0)
    time_at = lax.broadcasted_iota(jnp.int32, (width, 2 * LANE), 0)
    slot_at = lax.broadcasted_iota(jnp.int32, (width, 2 * LANE), 1)
    picked = jnp.where(time_at == PHASES * slot_at, 1.0, 0.0).astype(jnp.bfloat16)
    phased, squares = [], []
    for phase in range(PHASES):
        found = jnp.dot(
            ahead(window, phase).astype(jnp.bfloat16), picked, preferred_element_type=jnp.float32
        )
        phased.append(found)
        squares.append(
            sum(
                jnp.square(found[comp * local_sta : (comp + 1) * local_sta])
                for comp in range(comp_count)
            )
        )
    rows[...] = jnp.swapaxes(jnp.stack(phased + phased, axis=0), 0, 1)
    for phase, energy in enumerate(phase_energies(squares, span)):
        power[phase] = (1.0 / jnp.sqrt(energy * scale + eps))[:, :LANE]
    build_some(0, half + part)
    inbox[me] = parcels[me]
    for copy in copies:
        copy.wait()
    a_mine = a_base + row * near
    b_mine = b_base + column * narrow
    a_one, b_one = a_mine + column, b_mine + row
    chosen = [inbox[owners_ref[batch]].astype(jnp.float32) for batch in range(batch_count)]
    for at, skip in ((a_one, 0), (b_one, tmpl_count)):
        taps[at] = jnp.concatenate(
            [held[skip : skip + tmpl_count] for held in chosen], axis=0
        ).astype(jnp.bfloat16)

    def share(first, peer, count=1):
        held = taps.at[pl.ds(first, count)]
        return push(held, held, peer)

    b_row = share(b_one, row_peer)
    b_far = [share(b_one, peer) for peer in far_peers]
    a_far = [share(a_one, peer) for peer in far_peers]
    a_row = [share(a_one, row_peer)]
    early = [share(b_one, core_peer), share(a_one, core_peer)]
    build_some(half + part, local_sta - near)
    b_row.wait()
    b_other = b_mine + 1 - row
    b_far += [share(b_other, peer) for peer in far_peers]
    early.append(share(b_other, core_peer))
    build_some(local_sta - near, local_sta)
    for step in range(columns - 1):
        a_far[step].wait()
        arrived = a_mine + (column + columns - 1 - step) % columns
        a_row.append(share(arrived, row_peer))
        early.append(share(arrived, core_peer))
    running = (jnp.zeros((row_count, LANE), jnp.float32),) * PHASES
    running = score_some(a_mine, near, running)
    running = score_some(b_mine, narrow, running)
    for copy in early:
        copy.wait()
    twin = (1 - core) * half
    running = score_some(twin + row * near, near, running)
    running = score_some(twin + part + column * narrow, narrow, running)
    for copy in a_row + b_far:
        copy.wait()

    a_rest = (1 - row) * near
    rest = [(a_rest, near)] + [(part + other * narrow, narrow) for other in far]
    late = []
    for first, count in rest:
        late.append(share(base + first, core_peer, count))
    for first, count in rest:
        running = score_some(base + first, count, running)
    for copy in late:
        copy.wait()
    for first, count in rest:
        running = score_some(twin + first, count, running)

    kept = tmpl_count // 2
    for which in range(2):
        halves[which] = jnp.concatenate(
            [
                held[batch * tmpl_count + which * kept :][:kept]
                for held in running
                for batch in range(batch_count)
            ],
            axis=0,
        )
    copy = push(halves.at[1 - side], half_in, sta_peer)
    slot_at = lax.broadcasted_iota(jnp.int32, (LANE, stretch), 0)
    time_at = lax.broadcasted_iota(jnp.int32, (LANE, stretch), 1)
    copy.wait()
    summed = halves[side] + half_in[...]
    kept_rows = batch_count * kept
    result = jnp.zeros((kept_rows, stretch), jnp.float32)
    for phase in range(PHASES):
        placed = jnp.where(time_at == PHASES * slot_at + phase, 1.0, 0.0)
        result = result + jnp.dot(
            summed[phase * kept_rows : (phase + 1) * kept_rows],
            placed,
            precision=lax.Precision.HIGHEST,
            preferred_element_type=jnp.float32,
        )
    for batch in range(batch_count):
        out_ref[batch] = result[batch * kept : (batch + 1) * kept]


def network(slot, owners, data, moveouts, blocks):
    tmpl_count, comp_count, local_sta, span = slot.shape
    stretch = data.shape[2]
    batch_count = owners.shape[0]
    row_count = batch_count * tmpl_count
    depth = round_up(span, SUB)
    lanes = round_up(comp_count * depth, LANE)
    width = round_up(stretch + MAXM + depth, LANE)
    columns = blocks // 4
    tile = (row_count, lanes)
    count = blocks + 8 + 6 * columns
    kept = (batch_count, tmpl_count // 2, stretch)
    phased = (PHASES * row_count // 2, LANE)
    anywhere = pl.BlockSpec(memory_space=pl.ANY)
    in_vmem = pl.BlockSpec(memory_space=pltpu.VMEM)
    return pl.pallas_call(
        functools.partial(network_kernel, blocks),
        out_shape=jax.ShapeDtypeStruct(kept, jnp.float32),
        in_specs=[anywhere, pl.BlockSpec(memory_space=pltpu.SMEM), anywhere, anywhere],
        out_specs=in_vmem,
        scratch_shapes=[
            pltpu.VMEM(slot.shape, slot.dtype),
            pltpu.VMEM(data.shape, data.dtype),
            pltpu.VMEM(moveouts.shape, moveouts.dtype),
            pltpu.VMEM((local_sta,) + tile, jnp.bfloat16),
            pltpu.VMEM((blocks,) + tile, jnp.bfloat16),
            pltpu.VMEM((blocks,) + tile, jnp.bfloat16),
            pltpu.VMEM((comp_count, local_sta, width - stretch), jnp.bfloat16),
            pltpu.VMEM((comp_count * local_sta, 2 * PHASES, 2 * LANE), jnp.float32),
            pltpu.VMEM((PHASES, local_sta, LANE), jnp.float32),
            pltpu.VMEM((local_sta, row_count, LANE), jnp.int32),
            pltpu.VMEM((local_sta, lanes, LANE), jnp.bfloat16),
            pltpu.VMEM((2,) + phased, jnp.float32),
            pltpu.VMEM(phased, jnp.float32),
            pltpu.SemaphoreType.DMA((3,)),
            pltpu.SemaphoreType.DMA((count,)),
            pltpu.SemaphoreType.DMA((count,)),
        ],
        compiler_params=pltpu.CompilerParams(
            collective_id=0, has_side_effects=True, vmem_limit_bytes=60 * 1024 * 1024
        ),
    )(slot, owners, data, moveouts)


def spread_by_sum(slot, owners):
    span = slot.shape[3]
    depth = round_up(span, SUB)
    position = lax.axis_index("tm")
    batches = [jnp.where(owners[b] == position, slot, 0) for b in range(owners.shape[0])]
    taps = lax.psum(jnp.concatenate(batches, axis=2), "tm")
    taps = jnp.pad(taps[..., ::-1], ((0, 0), (0, 0), (0, 0), (depth - span, 0)))
    taps = jnp.concatenate(list(taps), axis=2)
    lanes = round_up(taps.shape[2], LANE)
    return jnp.pad(taps, ((0, 0), (0, 0), (0, lanes - taps.shape[2])))


def correlate_kernel(span, stretch, data_ref, taps_ref, lag_ref, out_ref, rows, power):
    local_sta, comp_count, width = data_ref.shape
    _, row_count, lanes = taps_ref.shape
    depth = round_up(span, SUB)
    reach = round_up(stretch + MAXM, LANE)
    scale = 1.0 / (comp_count * span)

    squares = jnp.zeros((local_sta, width), jnp.float32)
    for comp in range(comp_count):
        block = data_ref[:, comp, :].astype(jnp.float32)
        rows[comp] = block
        squares = squares + block * block
    energy = window_sums(squares, span) * scale
    power[...] = (1.0 / jnp.sqrt(energy + eps))[:, :reach]

    def station(index, running):
        pieces = []
        for comp in range(comp_count):
            record = jnp.broadcast_to(rows[comp, pl.ds(index, 1), :], (SUB, width))
            frames = pltpu.roll(record, width - (SUB - 1), axis=1, stride=1, stride_axis=0)
            frames = frames.astype(jnp.bfloat16)
            for start in range(depth - SUB, -1, -SUB):
                moved = frames if start == 0 else pltpu.roll(frames, width - start, axis=1)
                pieces.append(moved[:, :reach])
        while len(pieces) * SUB < lanes:
            pieces.append(jnp.zeros((SUB, reach), jnp.bfloat16))
        taps = taps_ref[index]
        products = jnp.dot(
            taps, jnp.concatenate(pieces, axis=0), preferred_element_type=jnp.float32
        )
        squared = jnp.square(taps.astype(jnp.float32))
        tmpl_power = jnp.sum(squared, axis=1, keepdims=True) * scale
        tmpl_scale = scale / jnp.sqrt(tmpl_power + eps)
        scores = products * power[pl.ds(index, 1), :] * tmpl_scale
        lags = lag_ref[index]
        step = 1
        while step <= MAXM:
            chosen = jnp.broadcast_to((lags & step)[:, :1] != 0, scores.shape)
            scores = jnp.where(chosen, pltpu.roll(scores, reach - step, axis=1), scores)
            step *= 2
        return running + scores[:, :stretch]

    out_ref[...] = lax.fori_loop(
        0, local_sta, station, jnp.zeros((row_count, stretch), jnp.float32), unroll=2
    )


def fits(data, bank, owners):
    local_sta, _, stretch = data.shape
    blocks = lax.axis_size("tm")
    row_count = owners.shape[0] * bank.shape[1]
    reach = round_up(bank.shape[-1], SUB) + MAXM
    return (
        lax.axis_size("sta") == 2
        and blocks % 4 == 0
        and blocks > 4
        and local_sta == 2 * blocks
        and row_count == SUB
        and owners.shape[0] == 2
        and bank.shape[1] % 2 == 0
        and stretch % LANE == 0
        and stretch >= round_up(reach, LANE)
        and stretch + MAXM <= PHASES * LANE
        and bank.shape[1] // 2 * owners.shape[0] % 8 == 0
        and bank.shape[-1] >= 4 * PHASES
        and reach - MAXM <= PHASES * LANE
    )


def shards(data, bank, owners, moveouts):
    local_sta, comp_count, stretch = data.shape
    span = bank.shape[-1]
    tmpl_count = bank.shape[1]
    batch_count = owners.shape[0]
    row_count = batch_count * tmpl_count
    blocks = lax.axis_size("tm")
    if fits(data, bank, owners):
        return network(
            jnp.transpose(bank[0], (0, 2, 1, 3)),
            owners,
            jnp.transpose(data, (1, 0, 2)),
            moveouts.reshape(row_count, local_sta),
            blocks,
        )

    edge = span - 1 + MAXM
    width = round_up(stretch + MAXM + round_up(span, SUB), LANE)
    reach = round_up(stretch + MAXM, LANE)
    route = [(i + 1, i) for i in range(blocks - 1)]
    edge_cells = lax.ppermute(data[:, :, :edge], "tm", route)
    taps = spread_by_sum(jnp.transpose(bank[0], (2, 1, 0, 3)), owners)
    window = jnp.concatenate([data, edge_cells], axis=2)
    window = jnp.pad(window, ((0, 0), (0, 0), (0, width - stretch - edge)))
    lags = jnp.transpose(moveouts, (2, 0, 1)).reshape(local_sta, row_count, 1)
    lags = jnp.broadcast_to(lags, (local_sta, row_count, LANE))
    partial_sum = pl.pallas_call(
        functools.partial(correlate_kernel, span, stretch),
        out_shape=jax.ShapeDtypeStruct((row_count, stretch), jnp.float32),
        in_specs=[pl.BlockSpec(memory_space=pltpu.VMEM)] * 3,
        out_specs=pl.BlockSpec(memory_space=pltpu.VMEM),
        scratch_shapes=[
            pltpu.VMEM((comp_count, local_sta, width), jnp.float32),
            pltpu.VMEM((local_sta, reach), jnp.float32),
        ],
        compiler_params=pltpu.CompilerParams(vmem_limit_bytes=32 * 1024 * 1024),
    )(window, taps, lags)
    partial_sum = partial_sum.reshape(batch_count, tmpl_count, stretch)
    return lax.psum_scatter(partial_sum, "sta", scatter_dimension=1, tiled=True)


def solution(mesh):
    placed = (P("sta", None, "tm"), P("tm", None, "sta", None, None), P(), P(None, None, "sta"))
    return jax.shard_map(
        shards, mesh=mesh, in_specs=placed, out_specs=P(None, "sta", "tm"), check_vma=False
    )
```

```python
import functools

import jax
import jax.numpy as jnp
from jax import lax
from jax.experimental import pallas as pl
from jax.experimental.pallas import tpu as pltpu
from jax.sharding import PartitionSpec as P

MAXM = 64
SUB = 16
LANE = 128
PHASES = 4

eps = 1e-06


def round_up(value, unit):
    return (value + unit - 1) // unit * unit


def window_sums(values, span):
    width = values.shape[-1]

    def ahead(block, distance):
        return pltpu.roll(block, width - distance, axis=1)

    total, done, size, run = None, 0, 1, values
    parts = []
    while size <= span:
        parts.append((size, run))
        if 2 * size <= span:
            run = run + ahead(run, size)
        size *= 2
    for size, run in reversed(parts):
        if done + size <= span:
            piece = run if done == 0 else ahead(run, done)
            total = piece if total is None else total + piece
            done += size
    return total


def laid_taps(slot_ref, lanes):
    tmpl_count, comp_count, local_sta, span = slot_ref.shape
    depth = round_up(span, SUB)
    lag_at = lax.broadcasted_iota(jnp.int32, (span, lanes), 0)
    slot_at = lax.broadcasted_iota(jnp.int32, (span, lanes), 1)
    taps = jnp.zeros((tmpl_count * local_sta, lanes), jnp.float32)
    for comp in range(comp_count):
        laid = jnp.where(slot_at == comp * depth + lag_at, 1.0, 0.0)
        block = slot_ref[:, comp].reshape(tmpl_count * local_sta, span)
        taps = taps + jnp.dot(
            block, laid.astype(jnp.bfloat16), preferred_element_type=jnp.float32
        )
    return jnp.swapaxes(taps.reshape(tmpl_count, local_sta, lanes), 0, 1)


def ahead(block, distance):
    width = block.shape[-1]
    return block if distance == 0 else pltpu.roll(block, width - distance, axis=block.ndim - 1)


def phase_energies(squares, span):
    inner_last = span // PHASES
    groups = sum(squares[1:], squares[0])
    inner, size, done, run = None, 1, 1, groups
    length = inner_last - 1
    while size <= length:
        if length & size:
            piece = ahead(run, done)
            inner = piece if inner is None else inner + piece
            done += size
        run = run + ahead(run, size)
        size *= 2
    energies = []
    for phase in range(PHASES):
        total = inner
        for step in range(phase, phase + span):
            at, which = step // PHASES, step % PHASES
            if not 1 <= at < inner_last:
                total = total + ahead(squares[which], at)
        energies.append(total)
    return energies


def network_kernel(
    blocks,
    slot_hbm,
    owners_ref,
    data_hbm,
    moveouts_hbm,
    out_ref,
    slot_ref,
    data_ref,
    moveouts_ref,
    taps,
    parcels,
    inbox,
    edge_in,
    rows,
    power,
    lags,
    frames,
    halves,
    half_in,
    local,
    send,
    recv,
):
    loads = [
        pltpu.make_async_copy(slot_hbm, slot_ref, local.at[0]),
        pltpu.make_async_copy(data_hbm, data_ref, local.at[1]),
        pltpu.make_async_copy(moveouts_hbm, moveouts_ref, local.at[2]),
    ]
    for load in loads:
        load.start()
    tmpl_count, comp_count, local_sta, span = slot_ref.shape
    lanes = taps.shape[2]
    stretch = data_ref.shape[2]
    width = stretch + edge_in.shape[2]
    batch_count = owners_ref.shape[0]
    row_count = batch_count * tmpl_count
    depth = round_up(span, SUB)
    scale = 1.0 / (comp_count * span)
    columns = blocks // 4
    me = lax.axis_index("tm")
    side = lax.axis_index("sta")
    core, row, column = me % 2, (me // 2) % 2, me // 4

    def place(at_column, at_row, at_core):
        return {"tm": (at_column * 2 + at_row) * 2 + at_core}

    core_peer = place(column, row, 1 - core)
    row_peer = place(column, 1 - row, core)
    far = [(column + step) % columns for step in range(1, columns)]
    far_peers = [place(other, row, core) for other in far]
    steps = sorted(range(1, blocks), key=lambda step: abs(2 * step - blocks))
    others = [(me + step) % blocks for step in steps]
    before = {"tm": (me + blocks - 1) % blocks}
    sta_peer = {"sta": 1 - side}

    barrier = pltpu.get_barrier_semaphore()
    peers = [sta_peer] + [{"tm": other} for other in others]
    for peer in peers:
        pl.semaphore_signal(
            barrier, inc=1, device_id=peer, device_id_type=pl.DeviceIdType.MESH
        )

    loads[0].wait()
    mine_taps = laid_taps(slot_ref, lanes)
    half = local_sta // 2
    part = half // 2
    near, narrow = part // 2, part // columns
    for other in range(blocks):
        at_core, at_row, at_column = other % 2, (other // 2) % 2, other // 4
        a_at = at_core * half + at_row * near + at_column
        b_at = at_core * half + part + at_column * narrow + at_row
        parcels[other] = jnp.concatenate([mine_taps[a_at], mine_taps[b_at]], axis=0).astype(
            jnp.bfloat16
        )

    pl.semaphore_wait(barrier, len(peers))
    used = [0]

    def push(source, target, peer):
        slot = used[0]
        used[0] += 1
        copy = pltpu.make_async_remote_copy(
            src_ref=source,
            dst_ref=target,
            send_sem=send.at[slot],
            recv_sem=recv.at[slot],
            device_id=peer,
            device_id_type=pl.DeviceIdType.MESH,
        )
        copy.start()
        return copy

    def build(index, unused):
        upper = lax.broadcasted_iota(jnp.int32, (2 * PHASES, 2 * LANE), 0) < PHASES
        for comp in range(comp_count):
            record = rows[comp * local_sta + index]
            groups = []
            for pair in range(SUB // (2 * PHASES)):
                groups.append(
                    jnp.where(upper, ahead(record, 2 * pair), ahead(record, 2 * pair + 1))
                )
            record = jnp.concatenate(groups, axis=0).astype(jnp.bfloat16)
            for group in range(depth // SUB):
                at = comp * depth + group * SUB
                frames[index, at : at + SUB, :] = ahead(record, group * SUB // PHASES)[:, :LANE]
        rest = lanes - comp_count * depth
        if rest > 0:
            frames[index, comp_count * depth :, :] = jnp.zeros((rest, LANE), jnp.bfloat16)
        return unused

    def score(index, running):
        station_taps = taps[index]
        moved = [station_taps]
        for phase in range(1, PHASES):
            moved.append(pltpu.roll(station_taps, phase, axis=1))
        products = jnp.dot(
            jnp.concatenate(moved, axis=0), frames[index], preferred_element_type=jnp.float32
        )
        squared = jnp.square(station_taps.astype(jnp.float32))
        tmpl_power = jnp.sum(squared, axis=1, keepdims=True) * scale
        tmpl_scale = scale / jnp.sqrt(tmpl_power + eps)
        scores = [
            products[phase * row_count : (phase + 1) * row_count]
            * power[phase, pl.ds(index, 1), :]
            * tmpl_scale
            for phase in range(PHASES)
        ]
        delays = lags[index]
        step = 1
        while step <= MAXM:
            chosen = (delays & step) != 0
            scores = [
                jnp.where(
                    chosen,
                    ahead(scores[(phase + step) % PHASES], (phase + step) // PHASES),
                    scores[phase],
                )
                for phase in range(PHASES)
            ]
            step *= 2
        return tuple(held + score for held, score in zip(running, scores))

    def build_some(first, last):
        lax.fori_loop(first, last, build, 0, unroll=4)

    def score_some(first, count, running):
        return lax.fori_loop(
            0, count, lambda i, held: score(first + i, held), running, unroll=min(count, 4)
        )

    base = core * half
    a_base, b_base = base, base + part

    loads[1].wait()
    edge_copy = push(data_ref.at[:, :, pl.ds(0, edge_in.shape[2])], edge_in, before)
    copies = [push(parcels.at[other], inbox.at[me], {"tm": other}) for other in others]
    loads[2].wait()
    delays = moveouts_ref[...]
    for station in range(local_sta):
        lags[station] = jnp.broadcast_to(delays[:, station : station + 1], (row_count, LANE))
    edge_copy.wait()
    pieces = []
    for comp in range(comp_count):
        edge = jnp.where(me == blocks - 1, 0.0, edge_in[comp].astype(jnp.float32))
        pieces.append(jnp.concatenate([data_ref[comp].astype(jnp.float32), edge], axis=1))
    window = jnp.concatenate(pieces, axis=0)
    time_at = lax.broadcasted_iota(jnp.int32, (width, 2 * LANE), 0)
    slot_at = lax.broadcasted_iota(jnp.int32, (width, 2 * LANE), 1)
    picked = jnp.where(time_at == PHASES * slot_at, 1.0, 0.0).astype(jnp.bfloat16)
    phased, squares = [], []
    for phase in range(PHASES):
        found = jnp.dot(
            ahead(window, phase).astype(jnp.bfloat16), picked, preferred_element_type=jnp.float32
        )
        phased.append(found)
        squares.append(
            sum(
                jnp.square(found[comp * local_sta : (comp + 1) * local_sta])
                for comp in range(comp_count)
            )
        )
    rows[...] = jnp.swapaxes(jnp.stack(phased + phased, axis=0), 0, 1)
    for phase, energy in enumerate(phase_energies(squares, span)):
        power[phase] = (1.0 / jnp.sqrt(energy * scale + eps))[:, :LANE]
    build_some(0, half + part)
    inbox[me] = parcels[me]
    for copy in copies:
        copy.wait()
    a_mine = a_base + row * near
    b_mine = b_base + column * narrow
    a_one, b_one = a_mine + column, b_mine + row
    chosen = [inbox[owners_ref[batch]].astype(jnp.float32) for batch in range(batch_count)]
    for at, skip in ((a_one, 0), (b_one, tmpl_count)):
        taps[at] = jnp.concatenate(
            [held[skip : skip + tmpl_count] for held in chosen], axis=0
        ).astype(jnp.bfloat16)

    def share(first, peer, count=1):
        held = taps.at[pl.ds(first, count)]
        return push(held, held, peer)

    b_row = share(b_one, row_peer)
    b_far = [share(b_one, peer) for peer in far_peers]
    a_far = [share(a_one, peer) for peer in far_peers]
    a_row = [share(a_one, row_peer)]
    early = [share(b_one, core_peer), share(a_one, core_peer)]
    build_some(half + part, local_sta - near)
    b_row.wait()
    b_other = b_mine + 1 - row
    b_far += [share(b_other, peer) for peer in far_peers]
    early.append(share(b_other, core_peer))
    build_some(local_sta - near, local_sta)
    for step in range(columns - 1):
        a_far[step].wait()
        arrived = a_mine + (column + columns - 1 - step) % columns
        a_row.append(share(arrived, row_peer))
        early.append(share(arrived, core_peer))
    running = (jnp.zeros((row_count, LANE), jnp.float32),) * PHASES
    running = score_some(a_mine, near, running)
    running = score_some(b_mine, narrow, running)
    for copy in early:
        copy.wait()
    twin = (1 - core) * half
    running = score_some(twin + row * near, near, running)
    running = score_some(twin + part + column * narrow, narrow, running)
    for copy in a_row + b_far:
        copy.wait()

    a_rest = (1 - row) * near
    rest = [(a_rest, near)] + [(part + other * narrow, narrow) for other in far]
    late = []
    for first, count in rest:
        late.append(share(base + first, core_peer, count))
    for first, count in rest:
        running = score_some(base + first, count, running)
    for copy in late:
        copy.wait()
    for first, count in rest:
        running = score_some(twin + first, count, running)

    kept = tmpl_count // 2
    for which in range(2):
        halves[which] = jnp.concatenate(
            [
                held[batch * tmpl_count + which * kept :][:kept]
                for held in running
                for batch in range(batch_count)
            ],
            axis=0,
        )
    copy = push(halves.at[1 - side], half_in, sta_peer)
    slot_at = lax.broadcasted_iota(jnp.int32, (LANE, stretch), 0)
    time_at = lax.broadcasted_iota(jnp.int32, (LANE, stretch), 1)
    copy.wait()
    summed = halves[side] + half_in[...]
    kept_rows = batch_count * kept
    result = jnp.zeros((kept_rows, stretch), jnp.float32)
    for phase in range(PHASES):
        placed = jnp.where(time_at == PHASES * slot_at + phase, 1.0, 0.0)
        result = result + jnp.dot(
            summed[phase * kept_rows : (phase + 1) * kept_rows],
            placed,
            precision=lax.Precision.HIGHEST,
            preferred_element_type=jnp.float32,
        )
    for batch in range(batch_count):
        out_ref[batch] = result[batch * kept : (batch + 1) * kept]


def network(slot, owners, data, moveouts, blocks):
    tmpl_count, comp_count, local_sta, span = slot.shape
    stretch = data.shape[2]
    batch_count = owners.shape[0]
    row_count = batch_count * tmpl_count
    depth = round_up(span, SUB)
    lanes = round_up(comp_count * depth, LANE)
    width = round_up(stretch + MAXM + depth, LANE)
    columns = blocks // 4
    tile = (row_count, lanes)
    count = blocks + 8 + 6 * columns
    kept = (batch_count, tmpl_count // 2, stretch)
    phased = (PHASES * row_count // 2, LANE)
    anywhere = pl.BlockSpec(memory_space=pl.ANY)
    in_vmem = pl.BlockSpec(memory_space=pltpu.VMEM)
    return pl.pallas_call(
        functools.partial(network_kernel, blocks),
        out_shape=jax.ShapeDtypeStruct(kept, jnp.float32),
        in_specs=[anywhere, pl.BlockSpec(memory_space=pltpu.SMEM), anywhere, anywhere],
        out_specs=in_vmem,
        scratch_shapes=[
            pltpu.VMEM(slot.shape, slot.dtype),
            pltpu.VMEM(data.shape, data.dtype),
            pltpu.VMEM(moveouts.shape, moveouts.dtype),
            pltpu.VMEM((local_sta,) + tile, jnp.bfloat16),
            pltpu.VMEM((blocks,) + tile, jnp.bfloat16),
            pltpu.VMEM((blocks,) + tile, jnp.bfloat16),
            pltpu.VMEM((comp_count, local_sta, width - stretch), jnp.bfloat16),
            pltpu.VMEM((comp_count * local_sta, 2 * PHASES, 2 * LANE), jnp.float32),
            pltpu.VMEM((PHASES, local_sta, LANE), jnp.float32),
            pltpu.VMEM((local_sta, row_count, LANE), jnp.int32),
            pltpu.VMEM((local_sta, lanes, LANE), jnp.bfloat16),
            pltpu.VMEM((2,) + phased, jnp.float32),
            pltpu.VMEM(phased, jnp.float32),
            pltpu.SemaphoreType.DMA((3,)),
            pltpu.SemaphoreType.DMA((count,)),
            pltpu.SemaphoreType.DMA((count,)),
        ],
        compiler_params=pltpu.CompilerParams(
            collective_id=0, has_side_effects=True, vmem_limit_bytes=60 * 1024 * 1024
        ),
    )(slot, owners, data, moveouts)


def spread_by_sum(slot, owners):
    span = slot.shape[3]
    depth = round_up(span, SUB)
    position = lax.axis_index("tm")
    batches = [jnp.where(owners[b] == position, slot, 0) for b in range(owners.shape[0])]
    taps = lax.psum(jnp.concatenate(batches, axis=2), "tm")
    taps = jnp.pad(taps[..., ::-1], ((0, 0), (0, 0), (0, 0), (depth - span, 0)))
    taps = jnp.concatenate(list(taps), axis=2)
    lanes = round_up(taps.shape[2], LANE)
    return jnp.pad(taps, ((0, 0), (0, 0), (0, lanes - taps.shape[2])))


def correlate_kernel(span, stretch, data_ref, taps_ref, lag_ref, out_ref, rows, power):
    local_sta, comp_count, width = data_ref.shape
    _, row_count, lanes = taps_ref.shape
    depth = round_up(span, SUB)
    reach = round_up(stretch + MAXM, LANE)
    scale = 1.0 / (comp_count * span)

    squares = jnp.zeros((local_sta, width), jnp.float32)
    for comp in range(comp_count):
        block = data_ref[:, comp, :].astype(jnp.float32)
        rows[comp] = block
        squares = squares + block * block
    energy = window_sums(squares, span) * scale
    power[...] = (1.0 / jnp.sqrt(energy + eps))[:, :reach]

    def station(index, running):
        pieces = []
        for comp in range(comp_count):
            record = jnp.broadcast_to(rows[comp, pl.ds(index, 1), :], (SUB, width))
            frames = pltpu.roll(record, width - (SUB - 1), axis=1, stride=1, stride_axis=0)
            frames = frames.astype(jnp.bfloat16)
            for start in range(depth - SUB, -1, -SUB):
                moved = frames if start == 0 else pltpu.roll(frames, width - start, axis=1)
                pieces.append(moved[:, :reach])
        while len(pieces) * SUB < lanes:
            pieces.append(jnp.zeros((SUB, reach), jnp.bfloat16))
        taps = taps_ref[index]
        products = jnp.dot(
            taps, jnp.concatenate(pieces, axis=0), preferred_element_type=jnp.float32
        )
        squared = jnp.square(taps.astype(jnp.float32))
        tmpl_power = jnp.sum(squared, axis=1, keepdims=True) * scale
        tmpl_scale = scale / jnp.sqrt(tmpl_power + eps)
        scores = products * power[pl.ds(index, 1), :] * tmpl_scale
        lags = lag_ref[index]
        step = 1
        while step <= MAXM:
            chosen = jnp.broadcast_to((lags & step)[:, :1] != 0, scores.shape)
            scores = jnp.where(chosen, pltpu.roll(scores, reach - step, axis=1), scores)
            step *= 2
        return running + scores[:, :stretch]

    out_ref[...] = lax.fori_loop(
        0, local_sta, station, jnp.zeros((row_count, stretch), jnp.float32), unroll=2
    )


def fits(data, bank, owners):
    local_sta, _, stretch = data.shape
    blocks = lax.axis_size("tm")
    row_count = owners.shape[0] * bank.shape[1]
    reach = round_up(bank.shape[-1], SUB) + MAXM
    return (
        lax.axis_size("sta") == 2
        and blocks % 4 == 0
        and blocks > 4
        and local_sta == 2 * blocks
        and row_count == SUB
        and owners.shape[0] == 2
        and bank.shape[1] % 2 == 0
        and stretch % LANE == 0
        and stretch >= round_up(reach, LANE)
        and stretch + MAXM <= PHASES * LANE
        and bank.shape[1] // 2 * owners.shape[0] % 8 == 0
        and bank.shape[-1] >= 4 * PHASES
        and reach - MAXM <= PHASES * LANE
    )


def shards(data, bank, owners, moveouts):
    local_sta, comp_count, stretch = data.shape
    span = bank.shape[-1]
    tmpl_count = bank.shape[1]
    batch_count = owners.shape[0]
    row_count = batch_count * tmpl_count
    blocks = lax.axis_size("tm")
    if fits(data, bank, owners):
        return network(
            jnp.transpose(bank[0], (0, 2, 1, 3)),
            owners,
            jnp.transpose(data, (1, 0, 2)),
            moveouts.reshape(row_count, local_sta),
            blocks,
        )

    edge = span - 1 + MAXM
    width = round_up(stretch + MAXM + round_up(span, SUB), LANE)
    reach = round_up(stretch + MAXM, LANE)
    route = [(i + 1, i) for i in range(blocks - 1)]
    edge_cells = lax.ppermute(data[:, :, :edge], "tm", route)
    taps = spread_by_sum(jnp.transpose(bank[0], (2, 1, 0, 3)), owners)
    window = jnp.concatenate([data, edge_cells], axis=2)
    window = jnp.pad(window, ((0, 0), (0, 0), (0, width - stretch - edge)))
    lags = jnp.transpose(moveouts, (2, 0, 1)).reshape(local_sta, row_count, 1)
    lags = jnp.broadcast_to(lags, (local_sta, row_count, LANE))
    partial_sum = pl.pallas_call(
        functools.partial(correlate_kernel, span, stretch),
        out_shape=jax.ShapeDtypeStruct((row_count, stretch), jnp.float32),
        in_specs=[pl.BlockSpec(memory_space=pltpu.VMEM)] * 3,
        out_specs=pl.BlockSpec(memory_space=pltpu.VMEM),
        scratch_shapes=[
            pltpu.VMEM((comp_count, local_sta, width), jnp.float32),
            pltpu.VMEM((local_sta, reach), jnp.float32),
        ],
        compiler_params=pltpu.CompilerParams(vmem_limit_bytes=32 * 1024 * 1024),
    )(window, taps, lags)
    partial_sum = partial_sum.reshape(batch_count, tmpl_count, stretch)
    return lax.psum_scatter(partial_sum, "sta", scatter_dimension=1, tiled=True)


def solution(mesh):
    placed = (P("sta", None, "tm"), P("tm", None, "sta", None, None), P(), P(None, None, "sta"))
    return jax.shard_map(
        shards, mesh=mesh, in_specs=placed, out_specs=P(None, "sta", "tm"), check_vma=False
    )
```
